256 devices in a mesh: slab: 8 (over z_lo, core), pencil: 32 (over z_hi, x, y).
Axes of the slice: x: 4, y: 4, z: 8 (z_hi: 2, z_lo: 4; z = z_hi * 4 + z_lo), core: 2. Of those that a mesh axis runs over, the one named last changes fastest.
Arguments:
- values: float32 [2, 1048576], P(None, ('slab', 'pencil')), may hold values from -6 to 6
- weights: float32 [16384, 4096], P(('slab', 'pencil')), may hold values from -1 to 2, as said below
- anchors: int32 [3, 16384], P(None, ('slab', 'pencil')), may hold values from 0 to 255, as said below
- counts: int32 [256], P(('slab', 'pencil')), may hold values from 16 to 64, as said below
- spectrum: float32 [256, 256, 256], P(('slab', 'pencil')), may hold values from 0.1 to 9, as said below
Outputs:
- matvec: float32 [2, 1048576], P(None, ('slab', 'pencil'))
The draws below stay inside these ranges and needn't reach their ends.
Inputs may be any that keep to these rules, and one draw needn't show every extreme that they name: The base cell of every block lies in the y range and z range of the device that holds the block: for slab index s and pencil index p, anchors[0] is in p * 8 to (p + 1) * 8 - 1 and anchors[1] is in s * 32 to (s + 1) * 32 - 1. A device's first counts blocks are live and the rest are padding slots; some device is full in every draw. `weights`: each row of 64 entries belongs to one observation. The spectrum equals its reflection: spectrum[i, j, l] = spectrum[(-i) mod 256, (-j) mod 256, (-l) mod 256].
All inputs are finite; a program needn't handle non-finite values.
Results may differ from the reference program's by a relative error of at most 0.00007.
Values sent between devices are 32-bit elements; how exact they have to be, the bound alone decides.
A program may use at most 192 MiB of HBM per device.

```python
import jax
import jax.numpy as jnp
from jax import lax

RHS = 2
GX = 256
GY = 256
GZ = 256
PATCH = 64
CUBE = 64
BLOCKS_DEV = 64
BLOCKS = 16384
OBS = 1048576
YCELLS = 8
ZCELLS = 32
N_SLAB = 8
N_PENCIL = 32


def keys_weights(shift):
    near = 1.5 * shift ** 3 - 2.5 * shift ** 2 + 1.0
    far = -0.5 * shift ** 3 + 2.5 * shift ** 2 - 4.0 * shift + 2.0
    return (near, far)


def draw_weights(key, part):
    key = jax.random.fold_in(key, 3)
    first, second = jax.random.split(key)
    frac = jax.random.uniform(first, (BLOCKS, PATCH, 3), jnp.float32)
    stacks = []
    for axis_pos in range(3):
        shift = frac[:, :, axis_pos]
        near_low, far_low = keys_weights(shift)
        near_high, far_high = keys_weights(1.0 - shift)
        far_low = -0.5 * (shift + 1.0) ** 3 + 2.5 * (shift + 1.0) ** 2 - 4.0 * (shift + 1.0) + 2.0
        far_high = -0.5 * (2.0 - shift) ** 3 + 2.5 * (2.0 - shift) ** 2 - 4.0 * (2.0 - shift) + 2.0
        stacks.append(jnp.stack([far_low, near_low, near_high, far_high], axis=-1))
    tensor = stacks[0][:, :, :, None, None] * stacks[1][:, :, None, :, None] * stacks[2][:, :, None, None, :]
    noise = 0.15 * jnp.clip(jax.random.normal(second, (BLOCKS, PATCH, CUBE), jnp.float32), -4.0, 4.0)
    return (tensor.reshape(BLOCKS, PATCH, CUBE) + noise).reshape(BLOCKS, PATCH * CUBE).astype(jnp.float32)


def draw_anchors(key, part):
    key = jax.random.fold_in(key, 5)
    first, second, third = jax.random.split(key, 3)
    block_ids = jnp.arange(BLOCKS, dtype=jnp.int32)
    device_ids = block_ids // BLOCKS_DEV
    slab_of = device_ids // N_PENCIL
    pencil_of = device_ids % N_PENCIL
    start_y = pencil_of * YCELLS + jax.random.randint(first, (BLOCKS,), 0, YCELLS)
    start_z = slab_of * ZCELLS + jax.random.randint(second, (BLOCKS,), 0, ZCELLS)
    start_x = jax.random.randint(third, (BLOCKS,), 0, GX)
    slot = block_ids % BLOCKS_DEV
    start_x = jnp.where(slot == 0, GX - 1, start_x)
    start_x = jnp.where(slot == 1, 0, start_x)
    return jnp.stack([start_y, start_z, start_x]).astype(jnp.int32)


def draw_counts(key, part):
    key = jax.random.fold_in(key, 7)
    first, second, third = jax.random.split(key, 3)
    devices = N_SLAB * N_PENCIL
    base = jax.random.randint(first, (devices,), BLOCKS_DEV // 4, BLOCKS_DEV + 1)
    full = jax.random.randint(second, (), 0, devices)
    lowest = (full + 1 + jax.random.randint(third, (), 0, devices - 1)) % devices
    places = jnp.arange(devices, dtype=jnp.int32)
    base = jnp.where(places == full, BLOCKS_DEV, base)
    base = jnp.where(places == lowest, BLOCKS_DEV // 4, base)
    return base.astype(jnp.int32)


def reflect(field):
    return jnp.roll(jnp.flip(field, (0, 1, 2)), 1, (0, 1, 2))


def spectrum_from(key, low, high, height):
    first, second = jax.random.split(key)
    rough_a = jax.random.uniform(first, (GX, GY, GZ), jnp.float32, low, high)
    rough_b = jax.random.uniform(second, (GX, GY, GZ), jnp.float32, low, high)
    rough_a = 0.5 * (rough_a + reflect(rough_a))
    rough_b = 0.5 * (rough_b + reflect(rough_b))
    freq_x = jnp.arange(GX, dtype=jnp.int32)
    freq_y = jnp.arange(GY, dtype=jnp.int32)
    freq_z = jnp.arange(GZ, dtype=jnp.int32)
    signed_x = jnp.minimum(freq_x, GX - freq_x).astype(jnp.float32) / GX
    signed_y = jnp.minimum(freq_y, GY - freq_y).astype(jnp.float32) / GY
    signed_z = jnp.minimum(freq_z, GZ - freq_z).astype(jnp.float32) / GZ
    radius = 256.0 * jnp.sqrt(signed_x[:, None, None] ** 2 + signed_y[None, :, None] ** 2 + signed_z[None, None, :] ** 2)
    matern = (1.0 + (radius / 3.0) ** 2) ** (-3.0)
    return 0.6 * rough_a + height * rough_b * matern


def draw_spectrum(key, part):
    key = jax.random.fold_in(key, 9)
    field = spectrum_from(key, 0.5, 1.5, 4.0)
    return field.astype(jnp.float32)


def steps_of(own_key, shape, cuts, low, top_value):
    loudness = 1.0
    for dim, parts in cuts:
        heights = jax.random.uniform(jax.random.fold_in(jax.random.fold_in(own_key, 6), dim), (parts,), jnp.float32, low / len(cuts), top_value / len(cuts))
        loudness = loudness * jnp.repeat(jnp.exp(heights), shape[dim] // parts).reshape((-1,) + (1,) * (len(shape) - 1 - dim))
    return loudness


def centred(stream_key, extent, spread, reach, shards=(), kind=jnp.bfloat16):
    loudness = steps_of(stream_key, extent, shards, -0.22, 0.18) if shards else 1.0
    values = jax.random.normal(stream_key, extent, jnp.float32) * spread * loudness
    return jnp.minimum(jnp.maximum(values, -reach), reach).astype(kind)


def setup_inputs(seed: int = 0) -> dict:
    arg_keys = jax.random.split(jax.random.key(seed), 6)
    return {
        "values": centred(arg_keys[0], (RHS, OBS), 1.0, 6.0, ((1, 256),), jnp.float32),
        "weights": draw_weights(jax.random.fold_in(arg_keys[5], 71), 0),
        "anchors": draw_anchors(jax.random.fold_in(arg_keys[5], 71), 0),
        "counts": draw_counts(jax.random.fold_in(arg_keys[5], 71), 0),
        "spectrum": draw_spectrum(jax.random.fold_in(arg_keys[5], 71), 0),
    }


def stencil_offsets():
    corner = jnp.arange(CUBE, dtype=jnp.int32)
    return corner // 16 - 1, (corner // 4) % 4 - 1, corner % 4 - 1


def reference(values, weights, anchors, counts, spectrum):
    block_ids = jnp.arange(BLOCKS, dtype=jnp.int32)
    device_ids = (block_ids // BLOCKS_DEV).astype(jnp.int32)
    live_mask = ((block_ids % BLOCKS_DEV) < counts[device_ids]).astype(jnp.float32)
    offset_y, offset_z, offset_x = stencil_offsets()
    cell_y = (anchors[0][:, None] + offset_y[None, :]) % GY
    cell_z = (anchors[1][:, None] + offset_z[None, :]) % GZ
    cell_x = (anchors[2][:, None] + offset_x[None, :]) % GX
    flat_cells = ((cell_y * GZ + cell_z) * GX + cell_x).reshape(-1).astype(jnp.int32)
    block_weights = weights.reshape(BLOCKS, PATCH, CUBE)
    observed = values.reshape(RHS, BLOCKS, PATCH)
    contrib = jnp.einsum("boc,rbo->rbc", block_weights, observed, precision=lax.Precision.HIGHEST)
    contrib = contrib * live_mask[None, :, None]
    grid_values = jnp.zeros((RHS, GY * GZ * GX), jnp.float32)
    grid_values = grid_values.at[:, flat_cells].add(contrib.reshape(RHS, -1))
    grid_values = grid_values.reshape(RHS, GY, GZ, GX)
    spectral = jnp.fft.fftn(grid_values, axes=(1, 2, 3))
    kernel_spec = jnp.transpose(spectrum, (1, 2, 0))
    smooth = jnp.real(jnp.fft.ifftn(spectral * kernel_spec[None], axes=(1, 2, 3))).astype(jnp.float32)
    picked = smooth.reshape(RHS, -1)[:, flat_cells].reshape(RHS, BLOCKS, CUBE)
    result = jnp.einsum("boc,rbc->rbo", block_weights, picked, precision=lax.Precision.HIGHEST)
    result = result * live_mask[None, :, None]
    return result.reshape(RHS, OBS)
```

```python
import math

import jax
import jax.numpy as jnp
import numpy as np
from jax import lax
from jax.experimental import pallas as pl
from jax.experimental.pallas import tpu as pltpu
from jax.sharding import PartitionSpec as P

MESH = pl.DeviceIdType.MESH
VM = pl.BlockSpec(memory_space=pltpu.VMEM)
SM = pl.BlockSpec(memory_space=pltpu.SMEM)
F32 = jnp.float32
BF16 = jnp.bfloat16
N = 256
LIMIT = 56 * 1024 * 1024


def halves(x):
    high = x.astype(BF16)
    low = (x - high.astype(F32)).astype(BF16)
    return high, low


def mm(a, b):
    return jnp.dot(a, b, preferred_element_type=F32)


def mm_nt(a, b):
    return lax.dot_general(a, b, (((1,), (1,)), ((), ())), preferred_element_type=F32)


def mm3(a_high, a_low, b_high, b_low):
    return mm(a_high, b_high) + (mm(a_high, b_low) + mm(a_low, b_high))


def np_halves(x):
    x = np.asarray(x, np.float32)
    high = x.astype(jnp.bfloat16)
    low = (x - high.astype(np.float32)).astype(jnp.bfloat16)
    return high, low


def here():
    s = lax.axis_index("slab")
    p = lax.axis_index("pencil")
    return s, p


def contrib_kernel(counts_ref, values_ref, weights_ref, anchor_ref, out_ref):
    lane = lax.broadcasted_iota(jnp.int32, (64, 128), 1)
    first = lane < 64
    totals = []
    for r in range(2):
        v = values_ref[r]
        total = jnp.zeros((64, 128), F32)
        for t in range(32):
            spread = jnp.where(first, v[:, 2 * t : 2 * t + 1], v[:, 2 * t + 1 : 2 * t + 2])
            total = total + weights_ref[:, t * 128 : (t + 1) * 128] * spread
        totals.append(total + pltpu.roll(total, 64, 1))
    both = jnp.where(first, totals[0], totals[1])
    row = lax.broadcasted_iota(jnp.int32, (64, 128), 0)
    both = jnp.where(row < counts_ref[0], both, 0.0)
    flipped = both.T
    for i in range(4):
        for j in range(4):
            for r in range(2):
                base = r * 64 + i * 16 + j * 4
                out_ref[i, r * 4 : r * 4 + 4, j * 64 : j * 64 + 64] = flipped[base : base + 4, :]
    out_ref[4] = anchor_ref[...]


def final_kernel(counts_ref, picked_ref, weights_ref, out_ref, flip_ref):
    for i in range(4):
        for j in range(4):
            for r in range(2):
                base = r * 64 + i * 16 + j * 4
                flip_ref[base : base + 4, :] = picked_ref[
                    i, r * 4 : r * 4 + 4, j * 64 : j * 64 + 64
                ]
    both = flip_ref[...].T
    lane = lax.broadcasted_iota(jnp.int32, (64, 128), 1)
    first = lane < 64
    row = lax.broadcasted_iota(jnp.int32, (64, 128), 0)
    both = jnp.where(row < counts_ref[0], both, 0.0)
    turned = pltpu.roll(both, 64, 1)
    picks = (jnp.where(first, both, turned), jnp.where(first, turned, both))
    total = jnp.zeros((128, 64), F32)
    source = lax.broadcasted_iota(jnp.int32, (256, 64), 0) // 64
    target = lax.broadcasted_iota(jnp.int32, (256, 64), 1)
    for t in range(16):
        left = weights_ref[:, t * 256 : t * 256 + 128]
        right = weights_ref[:, t * 256 + 128 : t * 256 + 256]
        product = jnp.concatenate(
            [jnp.concatenate([left * pk, right * pk], axis=1) for pk in picks], axis=0
        )
        high, low = halves(product)
        collect = (target == source + 4 * t).astype(F32).astype(BF16)
        total = total + mm(high, collect) + mm(low, collect)
    out_ref[0] = total[:64]
    out_ref[1] = total[64:]


def ring_place(z):
    return z // 4, lax.rem(z, 4)


def gather_kernel(x_ref, out_ref, ring_send, ring_recv, mate_send, mate_recv, own_sem):
    s, p = here()
    zl, c = s // 2, lax.rem(s, 2)
    zh, xy = p // 16, lax.rem(p, 16)
    z = zh * 4 + zl
    mate = (zl * 2 + 1 - c, p)

    def ring(t):
        h, l = ring_place(lax.rem(z + t, 8))
        return h, l, (l * 2 + c, h * 16 + xy)

    barrier = pltpu.get_barrier_semaphore()
    pl.semaphore_signal(barrier, inc=1, device_id=mate, device_id_type=MESH)
    for t in range(1, 8):
        pl.semaphore_signal(barrier, inc=1, device_id=ring(t)[2], device_id_type=MESH)
    pl.semaphore_wait(barrier, 8)
    ring_copies = []
    for t in (4, 5, 3, 6, 2, 7, 1):
        copy = pltpu.make_async_remote_copy(
            src_ref=x_ref,
            dst_ref=out_ref.at[zh, s],
            send_sem=ring_send.at[t],
            recv_sem=ring_recv.at[t],
            device_id=ring(t)[2],
            device_id_type=MESH,
        )
        copy.start()
        ring_copies.append((t, copy))
    mate_copies = []
    copy = pltpu.make_async_remote_copy(
        src_ref=x_ref,
        dst_ref=out_ref.at[zh, s],
        send_sem=mate_send.at[0],
        recv_sem=mate_recv.at[0],
        device_id=mate,
        device_id_type=MESH,
    )
    copy.start()
    mate_copies.append(copy)
    own = pltpu.make_async_copy(x_ref, out_ref.at[zh, s], own_sem)
    own.start()
    for t, ring_copy in ring_copies[::-1]:
        ring_copy.wait_recv()
        h, l, _ = ring(8 - t)
        copy = pltpu.make_async_remote_copy(
            src_ref=out_ref.at[h, l * 2 + c],
            dst_ref=out_ref.at[h, l * 2 + c],
            send_sem=mate_send.at[t],
            recv_sem=mate_recv.at[t],
            device_id=mate,
            device_id_type=MESH,
        )
        copy.start()
        mate_copies.append(copy)
    own.wait()
    for copy in mate_copies:
        copy.wait()
    for _, ring_copy in ring_copies:
        ring_copy.wait_send()


def plane_kernel(x_ref, out_ref, send_sem, recv_sem, own_sem):
    s, p = here()
    zh, xy = p // 16, lax.rem(p, 16)

    def other(t):
        to = lax.rem(xy + t, 16)
        return to, (s, zh * 16 + to)

    barrier = pltpu.get_barrier_semaphore()
    for t in range(1, 16):
        pl.semaphore_signal(barrier, inc=1, device_id=other(t)[1], device_id_type=MESH)
    pl.semaphore_wait(barrier, 15)
    copies = []
    for t in range(1, 16):
        to, device = other(t)
        copy = pltpu.make_async_remote_copy(
            src_ref=x_ref.at[:, pl.ds(to * 24, 24)],
            dst_ref=out_ref.at[:, pl.ds(xy * 24, 24)],
            send_sem=send_sem.at[t],
            recv_sem=recv_sem.at[t],
            device_id=device,
            device_id_type=MESH,
        )
        copy.start()
        copies.append(copy)
    mine = pl.ds(xy * 24, 24)
    own = pltpu.make_async_copy(x_ref.at[:, mine], out_ref.at[:, mine], own_sem)
    own.start()
    own.wait()
    for copy in copies:
        copy.wait()


def reduce_kernel(
    x_ref, out_ref, mate_buf, sum_buf, ring_buf, mate_send, mate_recv, ring_send, ring_recv
):
    s, p = here()
    zl, c = s // 2, lax.rem(s, 2)
    zh, xy = p // 16, lax.rem(p, 16)
    z = zh * 4 + zl
    mate = (zl * 2 + 1 - c, p)

    def ring(t):
        h, l = ring_place(lax.rem(z + t, 8))
        return h, l, (l * 2 + c, h * 16 + xy)

    barrier = pltpu.get_barrier_semaphore()
    pl.semaphore_signal(barrier, inc=1, device_id=mate, device_id_type=MESH)
    for t in range(1, 8):
        pl.semaphore_signal(barrier, inc=1, device_id=ring(t)[2], device_id_type=MESH)
    pl.semaphore_wait(barrier, 8)
    order = (4, 5, 3, 6, 2, 7, 1, 0)
    mate_copies = []
    for t in order:
        h, l, _ = ring(t)
        copy = pltpu.make_async_remote_copy(
            src_ref=x_ref.at[h, l * 2 + 1 - c],
            dst_ref=mate_buf.at[t],
            send_sem=mate_send.at[t],
            recv_sem=mate_recv.at[t],
            device_id=mate,
            device_id_type=MESH,
        )
        copy.start()
        mate_copies.append(copy)
    ring_copies = []
    for t, mate_copy in zip(order, mate_copies):
        mate_copy.wait_recv()
        h, l, device = ring(t)
        sum_buf[t] = x_ref[h, l * 2 + c] + mate_buf[t]
        if t:
            copy = pltpu.make_async_remote_copy(
                src_ref=sum_buf.at[t],
                dst_ref=ring_buf.at[t],
                send_sem=ring_send.at[t],
                recv_sem=ring_recv.at[t],
                device_id=device,
                device_id_type=MESH,
            )
            copy.start()
            ring_copies.append(copy)
    total = sum_buf[0]
    for t, copy in list(zip(order, ring_copies))[::-1]:
        copy.wait_recv()
        total = total + ring_buf[t]
    out_ref[...] = total
    for copy in ring_copies:
        copy.wait_send()
    for copy in mate_copies:
        copy.wait_send()


def circle(m):
    x = (jnp.bitwise_and(m, N - 1) - N // 2).astype(F32) * (math.pi / N)
    y = x * x
    sine = jnp.full_like(x, -1.0 / 39916800)
    for f in (362880, -5040, 120, -6, 1):
        sine = sine * y + 1.0 / f
    sine = sine * x
    cosine = jnp.full_like(x, 1.0 / 479001600)
    for f in (-3628800, 40320, -720, 24, -2, 1):
        cosine = cosine * y + 1.0 / f
    return 2.0 * sine * sine - 1.0, -2.0 * sine * cosine


def first_freq():
    s, p = here()
    return s * 32 + (p // 16) * 16


def phases(x_row, start):
    freq = lax.broadcasted_iota(jnp.int32, (16, N), 0) + start
    return circle(freq * x_row.astype(jnp.int32))


def spread_kernel(start_ref, g_ref, table_ref, out_ref, acc_ref):
    start = start_ref[0]
    grid_z = lax.broadcasted_iota(jnp.int32, (N, N), 0)
    out_ref[...] = jnp.zeros_like(out_ref)
    for zh in range(2):
        acc_ref[...] = jnp.zeros_like(acc_ref)

        def domain(s, carry):
            block = g_ref.at[zh, s]
            info = block[4]
            y_row, z_row, x_row = info[0:1], info[1:2], info[2:3]
            cosine, sine = phases(x_row, start)
            raw = jnp.concatenate([block[i] for i in range(4)], axis=1)
            high = raw.astype(BF16).astype(F32)
            low = raw - high
            stacked = jnp.concatenate([high, low, high, low], axis=0).astype(BF16)
            flat = mm(table_ref[...], stacked)
            parts = []
            for i in range(4):
                real = flat[:16, i * N : (i + 1) * N]
                imag = flat[16:, i * N : (i + 1) * N]
                parts.append(
                    jnp.concatenate(
                        [cosine * real + sine * imag, cosine * imag - sine * real], axis=0
                    )
                )
            y_all = jnp.broadcast_to(y_row, (32, N))
            highs, lows = [], []
            for yy in range(11):
                piece = jnp.zeros((32, N), F32)
                for i in range(4):
                    if 0 <= yy - i < 8:
                        piece = jnp.where(y_all == float(yy - i), parts[i], piece)
                h, l = halves(piece)
                highs.append(h)
                lows.append(l)
            hot = (grid_z == z_row.astype(jnp.int32)).astype(F32).astype(BF16)
            left = jnp.concatenate(highs, axis=0)
            right = jnp.concatenate(lows, axis=0)
            acc_ref[...] += mm_nt(left, hot) + mm_nt(right, hot)
            return carry

        lax.fori_loop(0, 8, domain, 0)
        for yy in range(11):
            for part in range(2):
                base = yy * 32 + part * 16
                for side in range(2):
                    out_ref[part * 2 + side, pl.ds(zh * 12 + yy, 16, stride=24), :] = acc_ref[
                        base : base + 16, side * 128 : side * 128 + 128
                    ]


def pick_kernel(start_ref, g_ref, smooth_ref, table_ref, out_ref, high_ref, low_ref):
    start = start_ref[0]
    grid_z = lax.broadcasted_iota(jnp.int32, (N, N), 0)
    for zh in range(2):
        for yy in range(11):
            for part in range(2):
                base = yy * 32 + part * 16
                for side in range(2):
                    piece = smooth_ref[part * 2 + side, pl.ds(zh * 12 + yy, 16, stride=24), :]
                    h, l = halves(piece)
                    high_ref[base : base + 16, side * 128 : side * 128 + 128] = h
                    low_ref[base : base + 16, side * 128 : side * 128 + 128] = l

        def domain(s, carry):
            info = g_ref[zh, s, 4]
            y_row, z_row, x_row = info[0:1], info[1:2], info[2:3]
            cosine, sine = phases(x_row, start)
            hot = (grid_z == z_row.astype(jnp.int32)).astype(F32).astype(BF16)
            rows = mm(high_ref[...], hot) + mm(low_ref[...], hot)
            y_all = jnp.broadcast_to(y_row, (32, N))
            turned = []
            for i in range(4):
                piece = rows[i * 32 : (i + 1) * 32]
                for y in range(1, 8):
                    piece = jnp.where(
                        y_all == float(y), rows[(y + i) * 32 : (y + i + 1) * 32], piece
                    )
                real, imag = piece[:16], piece[16:]
                turned.append(
                    jnp.concatenate(
                        [cosine * real - sine * imag, cosine * imag + sine * real], axis=0
                    )
                )
            flat = jnp.concatenate(turned, axis=1)
            high, low = halves(flat)
            stacked = jnp.concatenate([high, low, high, low], axis=0)
            picked = mm(table_ref[...], stacked)
            for i in range(4):
                out_ref[zh, s, i] = picked[:, i * N : (i + 1) * N]
            return carry

        lax.fori_loop(0, 8, domain, 0)


def filter_kernel(
    x_ref, spectrum_ref, yt_high, yt_low, zt_high, zt_low, yb_high, yb_low, out_ref
):
    fields = jnp.concatenate([x_ref[k] for k in range(4)], axis=1)
    b_high, b_low = halves(fields)
    u = mm3(yt_high[...], yt_low[...], b_high, b_low)
    real = u[:N, :N] + u[N:, N:]
    imag = u[:N, N:] - u[N:, :N]
    a_high, a_low = halves(jnp.concatenate([real, imag], axis=0))
    u = mm3(a_high, a_low, zt_high[...], zt_low[...])
    scale = spectrum_ref[0] * (1.0 / (N * N * N))
    real = (u[:N, :N] + u[N:, N:]) * scale
    imag = (u[N:, :N] - u[:N, N:]) * scale
    a_high, a_low = halves(jnp.concatenate([real, imag], axis=0))
    u = mm3(a_high, a_low, zt_high[...], zt_low[...])
    real = u[:N, :N] - u[N:, N:]
    imag = u[N:, :N] + u[:N, N:]
    b_high, b_low = halves(jnp.concatenate([real, imag], axis=1))
    u = mm3(yb_high[...], yb_low[...], b_high, b_low)
    real = u[:384, :N] - u[384:, N:]
    imag = u[:384, N:] + u[384:, :N]
    out_ref[0] = real[:, :128]
    out_ref[1] = real[:, 128:]
    out_ref[2] = imag[:, :128]
    out_ref[3] = imag[:, 128:]


def tables():
    row = np.arange(384)
    xy, zh, yy = row // 24, row // 12 % 2, row % 12
    y = ((zh * 16 + xy) * 8 - 1 + yy) % N
    used = (yy < 11).astype(np.float64)
    k = np.arange(N)
    angle = 2 * np.pi * (k[:, None] * y[None, :] % N) / N
    forward = np.concatenate([np.cos(angle) * used, np.sin(angle) * used], axis=0)
    backward = np.concatenate([np.cos(angle).T * used[:, None], np.sin(angle).T * used[:, None]], axis=0)
    angle = 2 * np.pi * (k[:, None] * k[None, :] % N) / N
    along = np.concatenate([np.cos(angle), np.sin(angle)], axis=1)
    return np_halves(forward), np_halves(along), np_halves(backward)


def params(ident=None):
    if ident is None:
        return pltpu.CompilerParams(vmem_limit_bytes=LIMIT)
    return pltpu.CompilerParams(
        collective_id=ident, has_side_effects=True, vmem_limit_bytes=LIMIT
    )


def call(kernel, shape, ins, scratch=(), ident=None):
    return pl.pallas_call(
        kernel,
        out_shape=jax.ShapeDtypeStruct(shape, F32),
        in_specs=ins,
        out_specs=VM,
        scratch_shapes=list(scratch),
        compiler_params=params(ident),
    )


DMA = pltpu.SemaphoreType.DMA


def plane(x, ident):
    return call(plane_kernel, x.shape, [VM], [DMA((16,)), DMA((16,)), DMA], ident)(x)


def on_device(values, weights, anchors, counts, spectrum):
    s, p = here()
    start = first_freq()
    y_rel = jnp.tile(anchors[0] - p * 8, 4)
    j = jnp.arange(256, dtype=jnp.int32) // 64
    z_row = (jnp.tile(anchors[1], 4) + j - 1) % N
    x_row = jnp.tile(anchors[2], 4)
    info = jnp.concatenate(
        [jnp.stack([y_rel, z_row, x_row]), jnp.zeros((5, N), jnp.int32)], axis=0
    ).astype(F32)
    start_arg = start.reshape(1).astype(jnp.int32)
    freq = start + jnp.arange(16, dtype=jnp.int32)
    offset = jnp.arange(4, dtype=jnp.int32) - 1
    angle = ((freq[:, None] * offset[None, :]) % N).astype(F32) * (2.0 * math.pi / N)
    cosine, sine = jnp.cos(angle), jnp.sin(angle)
    spread_table = jnp.concatenate(
        [jnp.concatenate([cosine, sine], 1), jnp.concatenate([-sine, cosine], 1)], 0
    )
    pick_table = spread_table.T
    sp_high = lax.reduce_precision(spread_table, 8, 7)
    sp_low = spread_table - sp_high
    pk_high, pk_low = sp_high.T, sp_low.T
    spread_table = jnp.concatenate([sp_high, sp_high, sp_low, sp_low], 1).astype(BF16)
    pick_table = jnp.concatenate([pk_high, pk_high, pk_low, pk_low], 1).astype(BF16)

    contrib = call(contrib_kernel, (5, 8, N), [SM, VM, VM, VM])(
        counts, values.reshape(2, 64, 64), weights, info
    )
    gathered = call(
        gather_kernel,
        (2, 8, 5, 8, N),
        [VM],
        [DMA((8,)), DMA((8,)), DMA((8,)), DMA((8,)), DMA],
        1,
    )(contrib)
    field = call(spread_kernel, (4, 384, 128), [SM, VM, VM], [pltpu.VMEM((352, N), F32)])(
        start_arg, gathered, spread_table
    )
    field = plane(field, 2)
    forward, along, backward = tables()
    smooth = call(filter_kernel, (4, 384, 128), [VM] * 8)(
        field, spectrum, *forward, *along, *backward
    )
    smooth = plane(smooth, 3)
    partial = call(
        pick_kernel,
        (2, 8, 4, 8, N),
        [SM, VM, VM, VM],
        [pltpu.VMEM((352, N), BF16), pltpu.VMEM((352, N), BF16)],
    )(start_arg, gathered, smooth, pick_table)
    picked = call(
        reduce_kernel,
        (4, 8, N),
        [VM],
        [pltpu.VMEM((8, 4, 8, N), F32)] * 3 + [DMA((8,))] * 4,
        4,
    )(partial)
    result = call(final_kernel, (2, 64, 64), [SM, VM, VM], [pltpu.VMEM((128, 64), F32)])(
        counts, picked, weights
    )
    return result.reshape(2, 64 * 64)


def solution(mesh):
    placed = (
        P(None, ("slab", "pencil")),
        P(("slab", "pencil"), None),
        P(None, ("slab", "pencil")),
        P(("slab", "pencil")),
        P(("slab", "pencil"), None, None),
    )
    return jax.shard_map(
        on_device,
        mesh=mesh,
        in_specs=placed,
        out_specs=P(None, ("slab", "pencil")),
        check_vma=False,
    )
```

```python
import math

import jax
import jax.numpy as jnp
import numpy as np
from jax import lax
from jax.experimental import pallas as pl
from jax.experimental.pallas import tpu as pltpu
from jax.sharding import PartitionSpec as P

MESH = pl.DeviceIdType.MESH
VM = pl.BlockSpec(memory_space=pltpu.VMEM)
SM = pl.BlockSpec(memory_space=pltpu.SMEM)
F32 = jnp.float32
BF16 = jnp.bfloat16
N = 256
LIMIT = 56 * 1024 * 1024


def halves(x):
    high = x.astype(BF16)
    low = (x - high.astype(F32)).astype(BF16)
    return high, low


def mm(a, b):
    return jnp.dot(a, b, preferred_element_type=F32)


def mm_nt(a, b):
    return lax.dot_general(a, b, (((1,), (1,)), ((), ())), preferred_element_type=F32)


def mm3(a_high, a_low, b_high, b_low):
    return mm(a_high, b_high) + (mm(a_high, b_low) + mm(a_low, b_high))


def np_halves(x):
    x = np.asarray(x, np.float32)
    high = x.astype(jnp.bfloat16)
    low = (x - high.astype(np.float32)).astype(jnp.bfloat16)
    return high, low


def circle(m):
    x = (jnp.bitwise_and(m, N - 1) - N // 2).astype(F32) * (math.pi / N)
    y = x * x
    sine = jnp.full_like(x, -1.0 / 39916800)
    for f in (362880, -5040, 120, -6, 1):
        sine = sine * y + 1.0 / f
    sine = sine * x
    cosine = jnp.full_like(x, 1.0 / 479001600)
    for f in (-3628800, 40320, -720, 24, -2, 1):
        cosine = cosine * y + 1.0 / f
    return 2.0 * sine * sine - 1.0, -2.0 * sine * cosine


def remote(src, dst, send, recv, device):
    return pltpu.make_async_remote_copy(
        src_ref=src, dst_ref=dst, send_sem=send, recv_sem=recv, device_id=device, device_id_type=MESH
    )


def offset_table(shape, start, spread):
    at0 = lax.broadcasted_iota(jnp.int32, shape, 0)
    at1 = lax.broadcasted_iota(jnp.int32, shape, 1)
    if spread:
        group, span = at0, at1
        piece, span = span // 8, lax.rem(span, 8)
    else:
        group, span = lax.rem(at1, 32), at0
        piece = at1 // 32
    part, freq = group // 16, lax.rem(group, 16) + start
    r, offset = span // 4, lax.rem(span, 4) - 1
    cosine, sine = circle(freq * offset)
    exact = jnp.where(part == r, cosine, jnp.where(part == 0, sine, -sine))
    high = exact.astype(BF16).astype(F32)
    return jnp.where(piece < 2, high, exact - high).astype(BF16)


def phases(x_row, start):
    freq = lax.broadcasted_iota(jnp.int32, (16, N), 0) + start
    return circle(freq * x_row.astype(jnp.int32))


def z_hot(z_row):
    grid_z = lax.broadcasted_iota(jnp.int32, (N, N), 0)
    return (grid_z == z_row.astype(jnp.int32)).astype(F32).astype(BF16)


def contributions(counts_ref, values_ref, weights_ref, waits, out_ref, flip_ref):
    for r in range(2):
        for b in range(64):
            flip_ref[r * 64 + b : r * 64 + b + 1, :] = values_ref[r : r + 1, b * 64 : b * 64 + 64]
    lane = lax.broadcasted_iota(jnp.int32, (64, 128), 1)
    first = lane < 64
    v = (flip_ref[:64, :], flip_ref[64:, :])
    totals = [jnp.zeros((64, 128), F32)] * 2
    for t in range(32):
        if t % 8 == 0:
            waits[t // 8].wait()
        tile = weights_ref[:, t * 128 : (t + 1) * 128]
        for r in range(2):
            spread = jnp.where(first, v[r][:, 2 * t : 2 * t + 1], v[r][:, 2 * t + 1 : 2 * t + 2])
            totals[r] = totals[r] + tile * spread
    totals = [t + pltpu.roll(t, 64, 1) for t in totals]
    both = jnp.where(first, totals[0], totals[1])
    row = lax.broadcasted_iota(jnp.int32, (64, 128), 0)
    both = jnp.where(row < counts_ref[0], both, 0.0)
    flipped = both.T
    for i in range(4):
        for j in range(4):
            for r in range(2):
                base = r * 64 + i * 16 + j * 4
                out_ref[i * 8 + r * 4 : i * 8 + r * 4 + 4, j * 64 : j * 64 + 64] = flipped[
                    base : base + 4, :
                ]


def results(counts_ref, picked, weights_ref, out_ref, flip_ref):
    for i in range(4):
        for j in range(4):
            for r in range(2):
                base = r * 64 + i * 16 + j * 4
                flip_ref[base : base + 4, :] = picked[i * 8 + r * 4 : i * 8 + r * 4 + 4, j * 64 : j * 64 + 64]
    both = flip_ref[...].T
    lane = lax.broadcasted_iota(jnp.int32, (64, 128), 1)
    first = lane < 64
    row = lax.broadcasted_iota(jnp.int32, (64, 128), 0)
    both = jnp.where(row < counts_ref[0], both, 0.0)
    turned = pltpu.roll(both, 64, 1)
    picks = (jnp.where(first, both, turned), jnp.where(first, turned, both))
    total = jnp.zeros((128, 64), F32)
    source = lax.broadcasted_iota(jnp.int32, (256, 64), 0) // 64
    target = lax.broadcasted_iota(jnp.int32, (256, 64), 1)
    for t in range(16):
        left = weights_ref[:, t * 256 : t * 256 + 128]
        right = weights_ref[:, t * 256 + 128 : t * 256 + 256]
        product = jnp.concatenate(
            [jnp.concatenate([left * pk, right * pk], axis=1) for pk in picks], axis=0
        )
        high, low = halves(product)
        collect = (target == source + 4 * t).astype(F32).astype(BF16)
        total = total + mm(high, collect) + mm(low, collect)
    for r in range(2):
        for b in range(64):
            out_ref[r : r + 1, b * 64 : b * 64 + 64] = total[r * 64 + b : r * 64 + b + 1, :]


def spread_domain(block_ref, table, start, acc_ref):
    info = block_ref[32:35]
    y_row, z_row, x_row = info[0:1], info[1:2], info[2:3]
    cosine, sine = phases(x_row, start)
    raw = jnp.concatenate([block_ref[i * 8 : i * 8 + 8] for i in range(4)], axis=1)
    high = raw.astype(BF16).astype(F32)
    low = raw - high
    stacked = jnp.concatenate([high, low, high, low], axis=0).astype(BF16)
    flat = mm(table, stacked)
    parts = []
    for i in range(4):
        real = flat[:16, i * N : (i + 1) * N]
        imag = flat[16:, i * N : (i + 1) * N]
        parts.append(
            jnp.concatenate([cosine * real + sine * imag, cosine * imag - sine * real], axis=0)
        )
    y_all = jnp.broadcast_to(y_row, (32, N))
    highs, lows = [], []
    for yy in range(11):
        piece = jnp.zeros((32, N), F32)
        for i in range(4):
            if 0 <= yy - i < 8:
                piece = jnp.where(y_all == float(yy - i), parts[i], piece)
        h, l = halves(piece)
        highs.append(h)
        lows.append(l)
    hot = z_hot(z_row)
    acc_ref[...] += mm_nt(jnp.concatenate(highs, axis=0), hot) + mm_nt(
        jnp.concatenate(lows, axis=0), hot
    )


def pick_domain(info, high, low, table, start):
    y_row, z_row, x_row = info[0:1], info[1:2], info[2:3]
    cosine, sine = phases(x_row, start)
    hot = z_hot(z_row)
    rows = mm(high, hot) + mm(low, hot)
    y_all = jnp.broadcast_to(y_row, (32, N))
    turned = []
    for i in range(4):
        piece = rows[i * 32 : (i + 1) * 32]
        for y in range(1, 8):
            piece = jnp.where(y_all == float(y), rows[(y + i) * 32 : (y + i + 1) * 32], piece)
        real, imag = piece[:16], piece[16:]
        turned.append(
            jnp.concatenate([cosine * real - sine * imag, cosine * imag + sine * real], axis=0)
        )
    h, l = halves(jnp.concatenate(turned, axis=1))
    return mm(table, jnp.concatenate([h, l, h, l], axis=0))


def whole_kernel(
    counts_ref,
    values_ref,
    anchors_ref,
    weights_any,
    spectrum_any,
    yt_any,
    zt_any,
    yb_any,
    out_ref,
    weights_ref,
    spectrum_ref,
    yt_ref,
    zt_ref,
    yb_ref,
    flip_ref,
    g_ref,
    acc_ref,
    field_ref,
    landed_ref,
    smooth_ref,
    back_ref,
    high_ref,
    low_ref,
    mate_out,
    mate_in,
    own_sum,
    ring_in,
    local_sem,
    ring_send,
    ring_recv,
    mate_send,
    mate_recv,
    to_send,
    to_recv,
    fro_send,
    fro_recv,
    ring2_send,
    ring2_recv,
    mate2_send,
    mate2_recv,
):
    s = lax.axis_index("slab")
    p = lax.axis_index("pencil")
    zl, c = s // 2, lax.rem(s, 2)
    zh, xy = p // 16, lax.rem(p, 16)
    z = zh * 4 + zl
    gx, gy = xy // 4, lax.rem(xy, 4)
    start = s * 32 + zh * 16
    mate = (zl * 2 + 1 - c, p)

    def ring(t):
        to = lax.rem(z + t, 8)
        h, l = to // 4, lax.rem(to, 4)
        return h, l, (l * 2 + c, h * 16 + xy)

    def chip(q, t):
        to = lax.rem(gx + q, 4) * 4 + lax.rem(gy + t, 4)
        return to, (s, zh * 16 + to)

    loads = []
    for k in range(4):
        cols = pl.ds(k * 1024, 1024)
        loads.append(
            pltpu.make_async_copy(weights_any.at[:, cols], weights_ref.at[:, cols], local_sem.at[k])
        )
    tables = [
        pltpu.make_async_copy(src, dst, local_sem.at[4 + k])
        for k, (src, dst) in enumerate(
            [
                (spectrum_any, spectrum_ref),
                (yt_any, yt_ref),
                (zt_any, zt_ref),
                (yb_any, yb_ref),
            ]
        )
    ]
    for load in loads + tables:
        load.start()
    landed_ref[...] = jnp.zeros_like(landed_ref)
    acc_ref[...] = jnp.zeros_like(acc_ref)

    others = [(q, t) for q in range(4) for t in range(4) if (q, t) != (0, 0)]
    barrier = pltpu.get_barrier_semaphore()
    pl.semaphore_signal(barrier, inc=1, device_id=mate, device_id_type=MESH)
    for t in range(1, 8):
        pl.semaphore_signal(barrier, inc=1, device_id=ring(t)[2], device_id_type=MESH)
    for q, t in others:
        pl.semaphore_signal(barrier, inc=1, device_id=chip(q, t)[1], device_id_type=MESH)

    mine = g_ref.at[zh, s]
    contributions(counts_ref, values_ref, weights_ref, loads, mine, flip_ref)
    mine[32:40, :] = jnp.zeros((8, N), F32)
    base_y = (anchors_ref[0:1, :] - p * 8).astype(F32)
    base_x = anchors_ref[2:3, :].astype(F32)
    for j in range(4):
        cols = slice(j * 64, j * 64 + 64)
        mine[32:33, cols] = base_y
        mine[33:34, cols] = jnp.bitwise_and(anchors_ref[1:2, :] + (j - 1), N - 1).astype(F32)
        mine[34:35, cols] = base_x
    pl.semaphore_wait(barrier, 23)


    def hand(h, d, t):
        place = g_ref.at[h, d]
        return remote(place, place, mate_send.at[t], mate_recv.at[t], mate)

    ring_copies = []
    for t in (1, 7, 2, 6, 3, 5, 4):
        place = g_ref.at[zh, s]
        copy = remote(place, place, ring_send.at[t], ring_recv.at[t], ring(t)[2])
        copy.start()
        ring_copies.append(copy)
    hand(zh, s, 0).start()
    table = offset_table((32, 32), start, True)

    def gather_step(k, carry):
        t = jnp.where(lax.rem(k, 2) == 1, (k + 1) // 2, lax.rem(8 - k // 2, 8))
        h, l, _ = ring(8 - t)
        d = l * 2 + c

        @pl.when(k > 0)
        def _():
            place = g_ref.at[h, d]
            remote(place, place, ring_send.at[t], ring_recv.at[t], mate).wait_recv()
            hand(h, d, t).start()

        spread_domain(g_ref.at[h, d], table, start, acc_ref.at[h])
        d = l * 2 + 1 - c
        hand(h, d, t).wait_recv()
        spread_domain(g_ref.at[h, d], table, start, acc_ref.at[h])
        return carry

    lax.fori_loop(0, 8, gather_step, 0)
    for copy in ring_copies:
        copy.wait_send()
    for t in range(8):
        hand(0, 0, t).wait_send()

    for h in range(2):
        for yy in range(11):
            for part in range(2):
                base = yy * 32 + part * 16
                for side in range(2):
                    field_ref[part * 2 + side, pl.ds(h * 11 + yy, 16, stride=24), :] = acc_ref[
                        h, base : base + 16, side * 128 : side * 128 + 128
                    ]
    sending = [(1, 0), (0, 1), (3, 0), (0, 3), (2, 0), (0, 2), (1, 1), (3, 3), (1, 3), (3, 1), (2, 2), (1, 2), (2, 1), (3, 2), (2, 3)]
    copies = []
    for q, t in sending:
        to, device = chip(q, t)
        k = q * 4 + t
        copy = remote(
            field_ref.at[:, pl.ds(to * 24, 22)],
            landed_ref.at[:, pl.ds(xy * 24, 22)],
            to_send.at[k],
            to_recv.at[k],
            device,
        )
        copy.start()
        copies.append(copy)
    own = pltpu.make_async_copy(
        field_ref.at[:, pl.ds(xy * 24, 22)], landed_ref.at[:, pl.ds(xy * 24, 22)], local_sem.at[8]
    )
    own.start()
    for load in tables:
        load.wait()
    own.wait()
    for copy in copies:
        copy.wait()

    fields = jnp.concatenate([landed_ref[k] for k in range(4)], axis=1)
    b_high, b_low = halves(fields)
    u = mm3(yt_ref[0], yt_ref[1], b_high, b_low)
    real = u[:N, :N] + u[N:, N:]
    imag = u[:N, N:] - u[N:, :N]
    a_high, a_low = halves(jnp.concatenate([real, imag], axis=0))
    u = mm3(a_high, a_low, zt_ref[0], zt_ref[1])
    scale = spectrum_ref[0] * (1.0 / (N * N * N))
    real = (u[:N, :N] + u[N:, N:]) * scale
    imag = (u[N:, :N] - u[:N, N:]) * scale
    a_high, a_low = halves(jnp.concatenate([real, imag], axis=0))
    u = mm3(a_high, a_low, zt_ref[0], zt_ref[1])
    real = u[:N, :N] - u[N:, N:]
    imag = u[N:, :N] + u[:N, N:]
    b_high, b_low = halves(jnp.concatenate([real, imag], axis=1))
    copies = []
    for q in (2, 1, 3, 0):
        column = lax.rem(gx + q, 4)
        u = mm3(yb_ref[0, column], yb_ref[1, column], b_high, b_low)
        real = u[:96, :N] - u[96:, N:]
        imag = u[:96, N:] + u[96:, :N]
        rows = pl.ds(column * 96, 96)
        smooth_ref[0, rows] = real[:, :128]
        smooth_ref[1, rows] = real[:, 128:]
        smooth_ref[2, rows] = imag[:, :128]
        smooth_ref[3, rows] = imag[:, 128:]
        for t in (1, 3, 2, 0):
            if (q, t) == (0, 0):
                continue
            to, device = chip(q, t)
            k = q * 4 + t
            copy = remote(
                smooth_ref.at[:, pl.ds(to * 24, 22)],
                back_ref.at[:, pl.ds(xy * 24, 22)],
                fro_send.at[k],
                fro_recv.at[k],
                device,
            )
            copy.start()
            copies.append(copy)
    own = pltpu.make_async_copy(
        smooth_ref.at[:, pl.ds(xy * 24, 22)], back_ref.at[:, pl.ds(xy * 24, 22)], local_sem.at[8]
    )
    own.start()
    table = offset_table((8, 128), start, False)
    own.wait()
    for copy in copies:
        copy.wait()
    for h in range(2):
        for yy in range(11):
            for part in range(2):
                base = yy * 32 + part * 16
                for side in range(2):
                    piece = back_ref[part * 2 + side, pl.ds(h * 11 + yy, 16, stride=24), :]
                    first, second = halves(piece)
                    high_ref[h, base : base + 16, side * 128 : side * 128 + 128] = first
                    low_ref[h, base : base + 16, side * 128 : side * 128 + 128] = second

    def order(k):
        return jnp.where(lax.rem(k, 2) == 0, 4 - k // 2, lax.rem(5 + k // 2, 8))

    def pass_on(k):
        return remote(mate_out.at[k], mate_in.at[k], mate2_send.at[k], mate2_recv.at[k], mate)

    def ring_on(k):
        t = order(k)
        return remote(own_sum.at[k], ring_in.at[t], ring2_send.at[t], ring2_recv.at[t], ring(t)[2])

    def pick(h, d):
        return pick_domain(g_ref[h, d, 32:35], high_ref[h], low_ref[h], table, start)

    def pick_step(k, carry):
        h, l, _ = ring(order(k))
        picked = pick(h, l * 2 + 1 - c)
        for i in range(4):
            mate_out[k, i * 8 : i * 8 + 8] = picked[:, i * N : (i + 1) * N]
        pass_on(k).start()
        picked = pick(h, l * 2 + c)
        for i in range(4):
            own_sum[k, i * 8 : i * 8 + 8] = picked[:, i * N : (i + 1) * N]

        @pl.when(k > 0)
        def _():
            pass_on(k - 1).wait_recv()
            own_sum[k - 1] = own_sum[k - 1] + mate_in[k - 1]
            ring_on(k - 1).start()

        return carry

    lax.fori_loop(0, 8, pick_step, 0)
    pass_on(7).wait_recv()
    total = own_sum[7] + mate_in[7]
    for k in range(7):
        t = (4, 5, 3, 6, 2, 7, 1)[k]
        remote(own_sum.at[k], ring_in.at[t], ring2_send.at[t], ring2_recv.at[t], mate).wait_recv()
        total = total + ring_in[t]
    results(counts_ref, total, weights_ref, out_ref, flip_ref)
    for k in range(8):
        pass_on(k).wait_send()
    for k in range(7):
        t = (4, 5, 3, 6, 2, 7, 1)[k]
        remote(own_sum.at[k], ring_in.at[t], ring2_send.at[t], ring2_recv.at[t], mate).wait_send()


def transform_tables():
    row = np.arange(384)
    xy, rest = row // 24, row % 24
    used = (rest < 22).astype(np.float64)
    y = ((rest // 11 * 16 + xy) * 8 - 1 + rest % 11) % N
    k = np.arange(N)
    angle = 2 * np.pi * (k[:, None] * y[None, :] % N) / N
    cosine, sine = np.cos(angle) * used, np.sin(angle) * used
    forward = np.concatenate([cosine, sine], axis=0)
    backward = np.concatenate([cosine.T.reshape(4, 96, N), sine.T.reshape(4, 96, N)], axis=1)
    angle = 2 * np.pi * (k[:, None] * k[None, :] % N) / N
    along = np.concatenate([np.cos(angle), np.sin(angle)], axis=1)
    return [np.stack(np_halves(x)) for x in (forward, along, backward)]


def on_device(values, weights, anchors, counts, spectrum):
    dma = pltpu.SemaphoreType.DMA
    anywhere = pl.BlockSpec(memory_space=pl.ANY)
    tables = transform_tables()
    field = pltpu.VMEM((4, 384, 128), F32)
    share = pltpu.VMEM((8, 32, N), F32)
    return pl.pallas_call(
        whole_kernel,
        out_shape=jax.ShapeDtypeStruct(values.shape, F32),
        in_specs=[SM, VM, VM] + [anywhere] * 5,
        out_specs=VM,
        scratch_shapes=[
            pltpu.VMEM(weights.shape, F32),
            pltpu.VMEM(spectrum.shape, F32),
            *[pltpu.VMEM(t.shape, BF16) for t in tables],
            pltpu.VMEM((128, 64), F32),
            pltpu.VMEM((2, 8, 40, N), F32),
            pltpu.VMEM((2, 352, N), F32),
            field,
            field,
            field,
            field,
            pltpu.VMEM((2, 352, N), BF16),
            pltpu.VMEM((2, 352, N), BF16),
            share,
            share,
            share,
            share,
            dma((9,)),
            *[dma((8,))] * 4,
            *[dma((16,))] * 4,
            *[dma((8,))] * 4,
        ],
        compiler_params=pltpu.CompilerParams(
            collective_id=1, has_side_effects=True, vmem_limit_bytes=LIMIT
        ),
    )(counts, values, anchors, weights, spectrum, *tables)


def solution(mesh):
    placed = (
        P(None, ("slab", "pencil")),
        P(("slab", "pencil"), None),
        P(None, ("slab", "pencil")),
        P(("slab", "pencil")),
        P(("slab", "pencil"), None, None),
    )
    return jax.shard_map(
        on_device,
        mesh=mesh,
        in_specs=placed,
        out_specs=P(None, ("slab", "pencil")),
        check_vma=False,
    )
```

```python
import math

import jax
import jax.numpy as jnp
import numpy as np
from jax import lax
from jax.experimental import pallas as pl
from jax.experimental.pallas import tpu as pltpu
from jax.sharding import PartitionSpec as P

MESH = pl.DeviceIdType.MESH
VM = pl.BlockSpec(memory_space=pltpu.VMEM)
SM = pl.BlockSpec(memory_space=pltpu.SMEM)
F32 = jnp.float32
BF16 = jnp.bfloat16
N = 256
LIMIT = 56 * 1024 * 1024


def halves(x):
    high = x.astype(BF16)
    low = (x - high.astype(F32)).astype(BF16)
    return high, low


def mm(a, b):
    return jnp.dot(a, b, preferred_element_type=F32)


def mm_nt(a, b):
    return lax.dot_general(a, b, (((1,), (1,)), ((), ())), preferred_element_type=F32)


def left3(high, low):
    return jnp.concatenate([high, high, low], axis=1)


def right3(high, low):
    return jnp.concatenate([high, low, high], axis=0)


def np_halves(x):
    x = np.asarray(x, np.float32)
    high = x.astype(jnp.bfloat16)
    low = (x - high.astype(np.float32)).astype(jnp.bfloat16)
    return high, low


def circle(m):
    x = (jnp.bitwise_and(m, N - 1) - N // 2).astype(F32) * (math.pi / N)
    y = x * x
    sine = jnp.full_like(x, -1.0 / 39916800)
    for f in (362880, -5040, 120, -6, 1):
        sine = sine * y + 1.0 / f
    sine = sine * x
    cosine = jnp.full_like(x, 1.0 / 479001600)
    for f in (-3628800, 40320, -720, 24, -2, 1):
        cosine = cosine * y + 1.0 / f
    return 2.0 * sine * sine - 1.0, -2.0 * sine * cosine


def remote(src, dst, send, recv, device):
    return pltpu.make_async_remote_copy(
        src_ref=src, dst_ref=dst, send_sem=send, recv_sem=recv, device_id=device, device_id_type=MESH
    )


def offset_table(shape, start, spread):
    at0 = lax.broadcasted_iota(jnp.int32, shape, 0)
    at1 = lax.broadcasted_iota(jnp.int32, shape, 1)
    if spread:
        group, span = at0, at1
        piece, span = span // 8, lax.rem(span, 8)
    else:
        group, span = lax.rem(at1, 32), at0
        piece = at1 // 32
    part, freq = group // 16, lax.rem(group, 16) + start
    r, offset = span // 4, lax.rem(span, 4) - 1
    cosine, sine = circle(freq * offset)
    exact = jnp.where(part == r, cosine, jnp.where(part == 0, sine, -sine))
    high = exact.astype(BF16).astype(F32)
    return jnp.where(piece < 2, high, exact - high).astype(BF16)


def phases(x_row, start):
    freq = lax.broadcasted_iota(jnp.int32, (16, N), 0) + start
    return circle(freq * x_row.astype(jnp.int32))


def z_hot(z_row):
    grid_z = lax.broadcasted_iota(jnp.int32, (N, N), 0)
    return (grid_z == z_row).astype(F32).astype(BF16)


def places(info):
    lane = lax.broadcasted_iota(jnp.int32, (8, 128), 1)
    first = lane < 64
    yz = jnp.broadcast_to(info[0:1], (8, 128))
    x = jnp.broadcast_to(info[1:2], (8, 128))
    zy = pltpu.roll(yz, 64, 1)
    y = jnp.where(first, yz, zy)
    z = jnp.where(first, zy, yz)
    x = jnp.where(first, x, pltpu.roll(x, 64, 1))
    y_row, z_row, x_row = (jnp.concatenate([v, v], axis=1)[0:1] for v in (y, z, x))
    j = lax.broadcasted_iota(jnp.int32, (1, N), 1) // 64
    z_row = jnp.bitwise_and(z_row.astype(jnp.int32) + (j - 1), N - 1)
    return y_row, z_row, x_row


def contributions(counts_ref, values_ref, weights_ref, waits, out_ref, flip_ref):
    for r in range(2):
        for b in range(64):
            flip_ref[r * 64 + b : r * 64 + b + 1, :] = values_ref[r : r + 1, b * 64 : b * 64 + 64]
    lane = lax.broadcasted_iota(jnp.int32, (64, 128), 1)
    first = lane < 64
    v = (flip_ref[:64, :], flip_ref[64:, :])
    totals = [jnp.zeros((64, 128), F32)] * 2
    for t in range(32):
        if t % 8 == 0:
            waits[t // 8].wait()
        tile = weights_ref[:, t * 128 : (t + 1) * 128]
        for r in range(2):
            spread = jnp.where(first, v[r][:, 2 * t : 2 * t + 1], v[r][:, 2 * t + 1 : 2 * t + 2])
            totals[r] = totals[r] + tile * spread
    totals = [t + pltpu.roll(t, 64, 1) for t in totals]
    both = jnp.where(first, totals[0], totals[1])
    row = lax.broadcasted_iota(jnp.int32, (64, 128), 0)
    both = jnp.where(row < counts_ref[0], both, 0.0)
    flipped = both.T
    for i in range(4):
        for j in range(4):
            for r in range(2):
                base = r * 64 + i * 16 + j * 4
                row = j // 2 * 32 + i * 8 + r * 4
                out_ref[row : row + 4, j % 2 * 64 : j % 2 * 64 + 64] = flipped[base : base + 4, :]


def results(counts_ref, picked, weights_ref, out_ref, flip_ref):
    for i in range(4):
        for j in range(4):
            for r in range(2):
                base = r * 64 + i * 16 + j * 4
                flip_ref[base : base + 4, :] = picked[i * 8 + r * 4 : i * 8 + r * 4 + 4, j * 64 : j * 64 + 64]
    both = flip_ref[...].T
    lane = lax.broadcasted_iota(jnp.int32, (64, 128), 1)
    first = lane < 64
    row = lax.broadcasted_iota(jnp.int32, (64, 128), 0)
    both = jnp.where(row < counts_ref[0], both, 0.0)
    turned = pltpu.roll(both, 64, 1)
    picks = (jnp.where(first, both, turned), jnp.where(first, turned, both))
    total = jnp.zeros((128, 64), F32)
    source = lax.broadcasted_iota(jnp.int32, (256, 64), 0) // 64
    target = lax.broadcasted_iota(jnp.int32, (256, 64), 1)
    for t in range(16):
        left = weights_ref[:, t * 256 : t * 256 + 128]
        right = weights_ref[:, t * 256 + 128 : t * 256 + 256]
        product = jnp.concatenate(
            [jnp.concatenate([left * pk, right * pk], axis=1) for pk in picks], axis=0
        )
        high, low = halves(product)
        collect = (target == source + 4 * t).astype(F32).astype(BF16)
        total = total + mm(high, collect) + mm(low, collect)
    for r in range(2):
        for b in range(64):
            out_ref[r : r + 1, b * 64 : b * 64 + 64] = total[r * 64 + b : r * 64 + b + 1, :]


def spread_domain(block_ref, table, start, acc_ref):
    y_row, z_row, x_row = places(block_ref[64:66])
    cosine, sine = phases(x_row, start)
    raw = jnp.concatenate(
        [block_ref[k * 32 + i * 8 : k * 32 + i * 8 + 8] for i in range(4) for k in range(2)], axis=1
    )
    high = raw.astype(BF16).astype(F32)
    low = raw - high
    stacked = jnp.concatenate([high, low, high, low], axis=0).astype(BF16)
    flat = mm(table, stacked)
    parts = []
    for i in range(4):
        real = flat[:16, i * N : (i + 1) * N]
        imag = flat[16:, i * N : (i + 1) * N]
        parts.append(
            jnp.concatenate([cosine * real + sine * imag, cosine * imag - sine * real], axis=0)
        )
    y_all = jnp.broadcast_to(y_row, (32, N))
    highs, lows = [], []
    for yy in range(11):
        piece = jnp.zeros((32, N), F32)
        for i in range(4):
            if 0 <= yy - i < 8:
                piece = jnp.where(y_all == float(yy - i), parts[i], piece)
        h, l = halves(piece)
        highs.append(h)
        lows.append(l)
    hot = z_hot(z_row)
    acc_ref[...] += mm_nt(jnp.concatenate(highs, axis=0), hot) + mm_nt(
        jnp.concatenate(lows, axis=0), hot
    )


def pick_domain(info, high, low, table, start):
    y_row, z_row, x_row = places(info)
    cosine, sine = phases(x_row, start)
    hot = z_hot(z_row)
    rows = mm(high, hot) + mm(low, hot)
    y_all = jnp.broadcast_to(y_row, (32, N))
    turned = []
    for i in range(4):
        piece = rows[i * 32 : (i + 1) * 32]
        for y in range(1, 8):
            piece = jnp.where(y_all == float(y), rows[(y + i) * 32 : (y + i + 1) * 32], piece)
        real, imag = piece[:16], piece[16:]
        turned.append(
            jnp.concatenate([cosine * real - sine * imag, cosine * imag + sine * real], axis=0)
        )
    h, l = halves(jnp.concatenate(turned, axis=1))
    return mm(table, jnp.concatenate([h, l, h, l], axis=0))


def whole_kernel(
    counts_ref,
    values_ref,
    anchors_ref,
    weights_any,
    spectrum_any,
    yt_any,
    zt_any,
    yb_any,
    out_ref,
    weights_ref,
    spectrum_ref,
    yt_ref,
    zt_ref,
    yb_ref,
    flip_ref,
    g_ref,
    acc_ref,
    field_ref,
    landed_ref,
    along_ref,
    smooth_ref,
    back_ref,
    high_ref,
    low_ref,
    mate_out,
    mate_in,
    own_sum,
    ring_in,
    local_sem,
    ring_send,
    ring_recv,
    mate_send,
    mate_recv,
    to_send,
    to_recv,
    fro_send,
    fro_recv,
    ring2_send,
    ring2_recv,
    mate2_send,
    mate2_recv,
):
    s = lax.axis_index("slab")
    p = lax.axis_index("pencil")
    zl, c = s // 2, lax.rem(s, 2)
    zh, xy = p // 16, lax.rem(p, 16)
    gx, gy = xy // 4, lax.rem(xy, 4)
    start = s * 32 + zh * 16
    mate = (zl * 2 + 1 - c, p)

    def chip(q, t):
        to = lax.rem(gx + q, 4) * 4 + lax.rem(gy + t, 4)
        return to, (s, zh * 16 + to)

    def ring_device(h, l):
        return l * 2 + c, h * 16 + xy

    loads = []
    for k in range(4):
        cols = pl.ds(k * 1024, 1024)
        loads.append(
            pltpu.make_async_copy(weights_any.at[:, cols], weights_ref.at[:, cols], local_sem.at[k])
        )
    tables = [
        pltpu.make_async_copy(src, dst, local_sem.at[4 + k])
        for k, (src, dst) in enumerate(
            [
                (spectrum_any, spectrum_ref),
                (yt_any, yt_ref),
                (zt_any, zt_ref),
                (yb_any, yb_ref),
            ]
        )
    ]
    for load in loads + tables:
        load.start()
    landed_ref[...] = jnp.zeros_like(landed_ref)
    acc_ref[...] = jnp.zeros_like(acc_ref)

    barrier = pltpu.get_barrier_semaphore()
    pl.semaphore_signal(barrier, inc=1, device_id=mate, device_id_type=MESH)
    for k in range(8):
        if k != 4:
            h, l = (1 - zh, lax.rem(zl + k, 4)) if k < 4 else (zh, lax.rem(zl + k - 4, 4))
            pl.semaphore_signal(barrier, inc=1, device_id=ring_device(h, l), device_id_type=MESH)
    others = [(q, t) for q in range(4) for t in range(4) if (q, t) != (0, 0)]
    for q, t in others:
        pl.semaphore_signal(barrier, inc=1, device_id=chip(q, t)[1], device_id_type=MESH)

    mine = g_ref.at[zh, s]
    contributions(counts_ref, values_ref, weights_ref, loads, mine, flip_ref)
    mine[64:65, :64] = (anchors_ref[0:1, :] - p * 8).astype(F32)
    mine[64:65, 64:] = anchors_ref[1:2, :].astype(F32)
    mine[65:66, :64] = anchors_ref[2:3, :].astype(F32)
    mine[65:66, 64:] = anchors_ref[2:3, :].astype(F32)
    pl.semaphore_wait(barrier, 23)

    def block(h, d):
        return g_ref.at[h, d, pl.ds(0, 66)]

    def hand(h, d, k):
        return remote(block(h, d), block(h, d), mate_send.at[k], mate_recv.at[k], mate)

    def source(k):
        same = k < 4
        h = jnp.where(same, zh, 1 - zh)
        return h, lax.rem(zl + 8 - k, 4) * 2 + c

    def arrive(k):
        h, d = source(k)
        remote(block(h, d), block(h, d), ring_send.at[k], ring_recv.at[k], mate).wait_recv()
        hand(h, d, k).start()

    ring_copies = []
    for k in (1, 3, 2, 5, 7, 6, 4):
        h, l = (zh, lax.rem(zl + k, 4)) if k < 4 else (1 - zh, lax.rem(zl + k - 4, 4))
        copy = remote(
            block(zh, s), block(zh, s), ring_send.at[k], ring_recv.at[k], ring_device(h, l)
        )
        copy.start()
        ring_copies.append(copy)
    hand(zh, s, 0).start()
    table = offset_table((32, 32), start, True)

    def gather_half(base, lead):
        def step(n, carry):
            k = base + lax.rem(n + lead, 4)
            h, d = source(k)
            spread_domain(g_ref.at[h, d], table, start, acc_ref)

            @pl.when(n < 3)
            def _():
                arrive(base + lax.rem(n + lead + 1, 4))

            d = d + 1 - 2 * c
            hand(h, d, k).wait_recv()
            spread_domain(g_ref.at[h, d], table, start, acc_ref)
            return carry

        lax.fori_loop(0, 4, step, 0)

    sending = [(1, 0), (0, 1), (3, 0), (0, 3), (2, 0), (0, 2), (1, 1), (3, 3), (1, 3), (3, 1)]
    sending += [(2, 2), (1, 2), (2, 1), (3, 2), (2, 3)]

    def rows_of(ref, h, to):
        return ref.at[h, :, pl.ds(to * 16, 11)]

    def send_half(turn, h):
        for yy in range(11):
            for part in range(2):
                base = yy * 32 + part * 16
                for side in range(2):
                    field_ref[h, part * 2 + side, pl.ds(yy, 16, stride=16), :] = acc_ref[
                        base : base + 16, side * 128 : side * 128 + 128
                    ]
        copies = []
        for q, t in sending:
            to, device = chip(q, t)
            k = q * 4 + t
            copy = remote(
                rows_of(field_ref, h, to),
                rows_of(landed_ref, h, xy),
                to_send.at[turn, k],
                to_recv.at[turn, k],
                device,
            )
            copy.start()
            copies.append(copy)
        own = pltpu.make_async_copy(
            rows_of(field_ref, h, xy), rows_of(landed_ref, h, xy), local_sem.at[8 + turn]
        )
        own.start()
        return copies, own

    gather_half(0, 0)
    first_copies, first_own = send_half(0, zh)
    acc_ref[...] = jnp.zeros_like(acc_ref)
    arrive(5)
    gather_half(4, 1)
    second_copies, second_own = send_half(1, 1 - zh)
    for copy in ring_copies:
        copy.wait_send()
    for k in range(8):
        hand(0, 0, k).wait_send()
    for load in tables:
        load.wait()

    def landed(h):
        return right3(*halves(jnp.concatenate([landed_ref[h, k] for k in range(4)], axis=1)))

    first_own.wait()
    for copy in first_copies:
        copy.wait()
    fields = landed(zh)
    for n in range(4):
        along_ref[n] = mm(left3(yt_ref[0, zh, n], yt_ref[1, zh, n]), fields)
    second_own.wait()
    for copy in second_copies:
        copy.wait()
    fields = landed(1 - zh)
    z_table = zt_ref[...]
    highs, lows = [], []
    for n in range(4):
        u = along_ref[n] + mm(left3(yt_ref[0, 1 - zh, n], yt_ref[1, 1 - zh, n]), fields)
        real = u[:64, :N] + u[64:, N:]
        imag = u[:64, N:] - u[64:, :N]
        u = mm(left3(*halves(jnp.concatenate([real, imag], axis=0))), z_table)
        scale = spectrum_ref[0, n * 64 : n * 64 + 64] * (1.0 / (N * N * N))
        real = (u[:64, :N] + u[64:, N:]) * scale
        imag = (u[64:, :N] - u[:64, N:]) * scale
        u = mm(left3(*halves(jnp.concatenate([real, imag], axis=0))), z_table)
        real = u[:64, :N] - u[64:, N:]
        imag = u[64:, :N] + u[:64, N:]
        h, l = halves(jnp.concatenate([real, imag], axis=1))
        highs.append(h)
        lows.append(l)
    fields = right3(jnp.concatenate(highs, axis=0), jnp.concatenate(lows, axis=0))

    def return_half(turn, h):
        copies = []
        for q in (2, 1, 3, 0):
            column = lax.rem(gx + q, 4)
            u = mm(left3(yb_ref[0, h, column], yb_ref[1, h, column]), fields)
            real = u[:64, :N] - u[64:, N:]
            imag = u[:64, N:] + u[64:, :N]
            rows = pl.ds(column * 64, 64)
            smooth_ref[h, 0, rows] = real[:, :128]
            smooth_ref[h, 1, rows] = real[:, 128:]
            smooth_ref[h, 2, rows] = imag[:, :128]
            smooth_ref[h, 3, rows] = imag[:, 128:]
            for t in (1, 3, 2, 0):
                if (q, t) == (0, 0):
                    continue
                to, device = chip(q, t)
                k = q * 4 + t
                copy = remote(
                    rows_of(smooth_ref, h, to),
                    rows_of(back_ref, h, xy),
                    fro_send.at[turn, k],
                    fro_recv.at[turn, k],
                    device,
                )
                copy.start()
                copies.append(copy)
        own = pltpu.make_async_copy(
            rows_of(smooth_ref, h, xy), rows_of(back_ref, h, xy), local_sem.at[8 + turn]
        )
        own.start()
        return copies, own

    first_copies, first_own = return_half(0, 1 - zh)
    second_copies, second_own = return_half(1, zh)
    table = offset_table((8, 128), start, False)

    def member(k):
        other = k < 4
        h = jnp.where(other, 1 - zh, zh)
        return h, jnp.where(other, lax.rem(zl + k, 4), lax.rem(zl + k + 1, 4))

    def pass_on(k):
        return remote(mate_out.at[k], mate_in.at[k], mate2_send.at[k], mate2_recv.at[k], mate)

    def ring_on(k):
        h, l = member(k)
        return remote(
            own_sum.at[k], ring_in.at[k], ring2_send.at[k], ring2_recv.at[k], ring_device(h, l)
        )

    def pick_half(copies, own, h, base):
        own.wait()
        for copy in copies:
            copy.wait()
        for yy in range(11):
            for part in range(2):
                row = yy * 32 + part * 16
                for side in range(2):
                    piece = back_ref[h, part * 2 + side, pl.ds(yy, 16, stride=16), :]
                    first, second = halves(piece)
                    high_ref[row : row + 16, side * 128 : side * 128 + 128] = first
                    low_ref[row : row + 16, side * 128 : side * 128 + 128] = second

        def pick(d):
            return pick_domain(g_ref[h, d, 64:66], high_ref[...], low_ref[...], table, start)

        def step(n, carry):
            k = base + n
            _, l = member(k)
            picked = pick(l * 2 + 1 - c)
            for i in range(4):
                mate_out[k, i * 8 : i * 8 + 8] = picked[:, i * N : (i + 1) * N]
            pass_on(k).start()
            picked = pick(l * 2 + c)
            for i in range(4):
                own_sum[k, i * 8 : i * 8 + 8] = picked[:, i * N : (i + 1) * N]

            @pl.when(k > 0)
            def _():
                pass_on(k - 1).wait_recv()
                own_sum[k - 1] = own_sum[k - 1] + mate_in[k - 1]
                ring_on(k - 1).start()

            return carry

        lax.fori_loop(0, 4, step, 0)

    pick_half(first_copies, first_own, 1 - zh, 0)
    pick_half(second_copies, second_own, zh, 4)
    pass_on(7).wait_recv()
    total = own_sum[7] + mate_in[7]
    for k in range(7):
        ring_on(k).wait_recv()
        total = total + ring_in[k]
    results(counts_ref, total, weights_ref, out_ref, flip_ref)
    for k in range(8):
        pass_on(k).wait_send()
    for k in range(7):
        ring_on(k).wait_send()


def transform_tables():
    row = np.arange(512)
    h, xy, yy = row // 256, row // 16 % 16, row % 16
    used = (yy < 11).astype(np.float64)
    y = ((h * 16 + xy) * 8 - 1 + yy) % N
    k = np.arange(N)
    angle = 2 * np.pi * (k[:, None] * y[None, :] % N) / N
    cosine, sine = np.cos(angle) * used, np.sin(angle) * used
    forward = np.stack([cosine.reshape(4, 64, 2, N), sine.reshape(4, 64, 2, N)], axis=1)
    forward = forward.transpose(3, 0, 1, 2, 4).reshape(2, 4, 128, N)
    backward = np.stack([cosine.T.reshape(2, 4, 64, N), sine.T.reshape(2, 4, 64, N)], axis=2)
    backward = backward.reshape(2, 4, 128, N)
    angle = 2 * np.pi * (k[:, None] * k[None, :] % N) / N
    high, low = np_halves(np.concatenate([np.cos(angle), np.sin(angle)], axis=1))
    along = np.concatenate([high, low, high], axis=0)
    return np.stack(np_halves(forward)), along, np.stack(np_halves(backward))


def on_device(values, weights, anchors, counts, spectrum):
    dma = pltpu.SemaphoreType.DMA
    anywhere = pl.BlockSpec(memory_space=pl.ANY)
    tables = transform_tables()
    field = pltpu.VMEM((2, 4, 256, 128), F32)
    share = pltpu.VMEM((8, 32, N), F32)
    return pl.pallas_call(
        whole_kernel,
        out_shape=jax.ShapeDtypeStruct(values.shape, F32),
        in_specs=[SM, VM, VM] + [anywhere] * 5,
        out_specs=VM,
        scratch_shapes=[
            pltpu.VMEM(weights.shape, F32),
            pltpu.VMEM(spectrum.shape, F32),
            *[pltpu.VMEM(t.shape, BF16) for t in tables],
            pltpu.VMEM((128, 64), F32),
            pltpu.VMEM((2, 8, 72, 128), F32),
            pltpu.VMEM((352, N), F32),
            field,
            field,
            pltpu.VMEM((4, 128, 2 * N), F32),
            field,
            field,
            pltpu.VMEM((352, N), BF16),
            pltpu.VMEM((352, N), BF16),
            share,
            share,
            share,
            share,
            dma((10,)),
            *[dma((8,))] * 4,
            *[dma((2, 16))] * 4,
            *[dma((8,))] * 4,
        ],
        compiler_params=pltpu.CompilerParams(
            collective_id=1, has_side_effects=True, vmem_limit_bytes=LIMIT
        ),
    )(counts, values, anchors, weights, spectrum, *tables)


def solution(mesh):
    placed = (
        P(None, ("slab", "pencil")),
        P(("slab", "pencil"), None),
        P(None, ("slab", "pencil")),
        P(("slab", "pencil")),
        P(("slab", "pencil"), None, None),
    )
    return jax.shard_map(
        on_device,
        mesh=mesh,
        in_specs=placed,
        out_specs=P(None, ("slab", "pencil")),
        check_vma=False,
    )
```

```python
import math

import jax
import jax.numpy as jnp
import numpy as np
from jax import lax
from jax.experimental import pallas as pl
from jax.experimental.pallas import tpu as pltpu
from jax.sharding import PartitionSpec as P

MESH = pl.DeviceIdType.MESH
VM = pl.BlockSpec(memory_space=pltpu.VMEM)
SM = pl.BlockSpec(memory_space=pltpu.SMEM)
F32 = jnp.float32
BF16 = jnp.bfloat16
N = 256
LIMIT = 56 * 1024 * 1024


def halves(x):
    high = x.astype(BF16)
    low = (x - high.astype(F32)).astype(BF16)
    return high, low


def mm(a, b):
    return jnp.dot(a, b, preferred_element_type=F32)


def mm_nt(a, b):
    return lax.dot_general(a, b, (((1,), (1,)), ((), ())), preferred_element_type=F32)


def left3(high, low):
    return jnp.concatenate([high, high, low], axis=1)


def right3(high, low):
    return jnp.concatenate([high, low, high], axis=0)


def np_halves(x):
    x = np.asarray(x, np.float32)
    high = x.astype(jnp.bfloat16)
    low = (x - high.astype(np.float32)).astype(jnp.bfloat16)
    return high, low


def circle(m):
    x = (jnp.bitwise_and(m, N - 1) - N // 2).astype(F32) * (math.pi / N)
    y = x * x
    sine = jnp.full_like(x, -1.0 / 39916800)
    for f in (362880, -5040, 120, -6, 1):
        sine = sine * y + 1.0 / f
    sine = sine * x
    cosine = jnp.full_like(x, 1.0 / 479001600)
    for f in (-3628800, 40320, -720, 24, -2, 1):
        cosine = cosine * y + 1.0 / f
    return 2.0 * sine * sine - 1.0, -2.0 * sine * cosine


def remote(src, dst, send, recv, device):
    return pltpu.make_async_remote_copy(
        src_ref=src, dst_ref=dst, send_sem=send, recv_sem=recv, device_id=device, device_id_type=MESH
    )


def offset_table(shape, start, spread):
    at0 = lax.broadcasted_iota(jnp.int32, shape, 0)
    at1 = lax.broadcasted_iota(jnp.int32, shape, 1)
    if spread:
        group, span = at0, at1
        piece, span = span // 8, lax.rem(span, 8)
    else:
        group, span = lax.rem(at1, 32), at0
        piece = at1 // 32
    part, freq = group // 16, lax.rem(group, 16) + start
    r, offset = span // 4, lax.rem(span, 4) - 1
    cosine, sine = circle(freq * offset)
    exact = jnp.where(part == r, cosine, jnp.where(part == 0, sine, -sine))
    high = exact.astype(BF16).astype(F32)
    return jnp.where(piece < 2, high, exact - high).astype(BF16)


def phases(x_row, start):
    freq = lax.broadcasted_iota(jnp.int32, (16, x_row.shape[1]), 0) + start
    return circle(freq * x_row.astype(jnp.int32))


def z_hot(z_row):
    grid_z = lax.broadcasted_iota(jnp.int32, (N, z_row.shape[1]), 0)
    return (grid_z == z_row).astype(F32).astype(BF16)


def places(info):
    lane = lax.broadcasted_iota(jnp.int32, (8, 128), 1)
    first = lane < 64
    yz = jnp.broadcast_to(info[0:1], (8, 128))
    x = jnp.broadcast_to(info[1:2], (8, 128))
    zy = pltpu.roll(yz, 64, 1)
    y = jnp.where(first, yz, zy)
    z = jnp.where(first, zy, yz)
    x = jnp.where(first, x, pltpu.roll(x, 64, 1))
    y_row, z_row, x_row = (jnp.concatenate([v, v], axis=1)[0:1] for v in (y, z, x))
    j = lax.broadcasted_iota(jnp.int32, (1, N), 1) // 64
    z_row = jnp.bitwise_and(z_row.astype(jnp.int32) + (j - 1), N - 1)
    return y_row, z_row, x_row


def contributions(counts_ref, values_ref, weights_ref, waits, out_ref, flip_ref):
    for r in range(2):
        for b in range(64):
            flip_ref[r * 64 + b : r * 64 + b + 1, :] = values_ref[r : r + 1, b * 64 : b * 64 + 64]
    lane = lax.broadcasted_iota(jnp.int32, (64, 128), 1)
    first = lane < 64
    v = (flip_ref[:64, :], flip_ref[64:, :])
    totals = [jnp.zeros((64, 128), F32)] * 2
    for t in range(32):
        if t % 8 == 0:
            waits[t // 8].wait()
        tile = weights_ref[:, t * 128 : (t + 1) * 128]
        for r in range(2):
            spread = jnp.where(first, v[r][:, 2 * t : 2 * t + 1], v[r][:, 2 * t + 1 : 2 * t + 2])
            totals[r] = totals[r] + tile * spread
    totals = [t + pltpu.roll(t, 64, 1) for t in totals]
    both = jnp.where(first, totals[0], totals[1])
    row = lax.broadcasted_iota(jnp.int32, (64, 128), 0)
    both = jnp.where(row < counts_ref[0], both, 0.0)
    flipped = both.T
    for i in range(4):
        for j in range(4):
            for r in range(2):
                base = r * 64 + i * 16 + j * 4
                row = j // 2 * 32 + i * 8 + r * 4
                out_ref[row : row + 4, j % 2 * 64 : j % 2 * 64 + 64] = flipped[base : base + 4, :]


def results(counts_ref, picked, weights_ref, out_ref, flip_ref):
    for i in range(4):
        for j in range(4):
            for r in range(2):
                base = r * 64 + i * 16 + j * 4
                flip_ref[base : base + 4, :] = picked[i * 8 + r * 4 : i * 8 + r * 4 + 4, j * 64 : j * 64 + 64]
    both = flip_ref[...].T
    lane = lax.broadcasted_iota(jnp.int32, (64, 128), 1)
    first = lane < 64
    row = lax.broadcasted_iota(jnp.int32, (64, 128), 0)
    both = jnp.where(row < counts_ref[0], both, 0.0)
    turned = pltpu.roll(both, 64, 1)
    picks = (jnp.where(first, both, turned), jnp.where(first, turned, both))
    total = jnp.zeros((128, 64), F32)
    source = lax.broadcasted_iota(jnp.int32, (256, 64), 0) // 64
    target = lax.broadcasted_iota(jnp.int32, (256, 64), 1)
    for t in range(16):
        left = weights_ref[:, t * 256 : t * 256 + 128]
        right = weights_ref[:, t * 256 + 128 : t * 256 + 256]
        product = jnp.concatenate(
            [jnp.concatenate([left * pk, right * pk], axis=1) for pk in picks], axis=0
        )
        high, low = halves(product)
        collect = (target == source + 4 * t).astype(F32).astype(BF16)
        total = total + mm(high, collect) + mm(low, collect)
    for r in range(2):
        for b in range(64):
            out_ref[r : r + 1, b * 64 : b * 64 + 64] = total[r * 64 + b : r * 64 + b + 1, :]


def spread_pair(blocks, table, start, acc_ref):
    rows = [places(b[64:66]) for b in blocks]
    y_row, z_row, x_row = (jnp.concatenate([r[k] for r in rows], axis=1) for k in range(3))
    cosine, sine = phases(x_row, start)
    raw = jnp.concatenate(
        [
            b[k * 32 + i * 8 : k * 32 + i * 8 + 8]
            for i in range(4)
            for b in blocks
            for k in range(2)
        ],
        axis=1,
    )
    high = raw.astype(BF16).astype(F32)
    low = raw - high
    stacked = jnp.concatenate([high, low, high, low], axis=0).astype(BF16)
    flat = mm(table, stacked)
    parts = []
    for i in range(4):
        real = flat[:16, i * 2 * N : (i + 1) * 2 * N]
        imag = flat[16:, i * 2 * N : (i + 1) * 2 * N]
        parts.append(
            jnp.concatenate([cosine * real + sine * imag, cosine * imag - sine * real], axis=0)
        )
    y_all = jnp.broadcast_to(y_row, (32, 2 * N))
    pieces = []
    for yy in range(11):
        piece = jnp.zeros((32, 2 * N), F32)
        for i in range(4):
            if 0 <= yy - i < 8:
                piece = jnp.where(y_all == float(yy - i), parts[i], piece)
        pieces.append(jnp.concatenate(halves(piece), axis=1))
    hot = z_hot(z_row)
    acc_ref[...] += mm_nt(jnp.concatenate(pieces, axis=0), jnp.concatenate([hot, hot], axis=1))


def pick_pair(infos, smooth, table, start):
    rows = [places(info) for info in infos]
    y_row, z_row, x_row = (jnp.concatenate([r[k] for r in rows], axis=1) for k in range(3))
    cosine, sine = phases(x_row, start)
    hot = z_hot(z_row)
    rows = mm(smooth, jnp.concatenate([hot, hot], axis=0))
    y_all = jnp.broadcast_to(y_row, (32, 2 * N))
    turned = []
    for i in range(4):
        piece = rows[i * 32 : (i + 1) * 32]
        for y in range(1, 8):
            piece = jnp.where(y_all == float(y), rows[(y + i) * 32 : (y + i + 1) * 32], piece)
        real, imag = piece[:16], piece[16:]
        turned.append(
            jnp.concatenate([cosine * real - sine * imag, cosine * imag + sine * real], axis=0)
        )
    h, l = halves(jnp.concatenate(turned, axis=1))
    return mm(table, jnp.concatenate([h, l, h, l], axis=0))


def whole_kernel(
    counts_ref,
    values_ref,
    anchors_ref,
    weights_any,
    spectrum_any,
    yt_any,
    zt_any,
    yb_any,
    out_ref,
    weights_ref,
    spectrum_ref,
    yt_ref,
    zt_ref,
    yb_ref,
    flip_ref,
    g_ref,
    acc_ref,
    field_ref,
    landed_ref,
    along_ref,
    smooth_ref,
    back_ref,
    pair_ref,
    mate_out,
    mate_in,
    own_sum,
    ring_in,
    local_sem,
    ring_send,
    ring_recv,
    mate_send,
    mate_recv,
    to_send,
    to_recv,
    fro_send,
    fro_recv,
    ring2_send,
    ring2_recv,
    mate2_send,
    mate2_recv,
):
    s = lax.axis_index("slab")
    p = lax.axis_index("pencil")
    zl, c = s // 2, lax.rem(s, 2)
    zh, xy = p // 16, lax.rem(p, 16)
    gx, gy = xy // 4, lax.rem(xy, 4)
    start = s * 32 + zh * 16
    mate = (zl * 2 + 1 - c, p)

    def chip(q, t):
        to = lax.rem(gx + q, 4) * 4 + lax.rem(gy + t, 4)
        return to, (s, zh * 16 + to)

    def ring_device(h, l):
        return l * 2 + c, h * 16 + xy

    loads = []
    for k in range(4):
        cols = pl.ds(k * 1024, 1024)
        loads.append(
            pltpu.make_async_copy(weights_any.at[:, cols], weights_ref.at[:, cols], local_sem.at[k])
        )
    tables = [
        pltpu.make_async_copy(src, dst, local_sem.at[4 + k])
        for k, (src, dst) in enumerate(
            [
                (spectrum_any, spectrum_ref),
                (yt_any, yt_ref),
                (zt_any, zt_ref),
                (yb_any, yb_ref),
            ]
        )
    ]
    for load in loads + tables:
        load.start()
    landed_ref[...] = jnp.zeros_like(landed_ref)
    acc_ref[...] = jnp.zeros_like(acc_ref)

    barrier = pltpu.get_barrier_semaphore()
    pl.semaphore_signal(barrier, inc=1, device_id=mate, device_id_type=MESH)
    for k in range(8):
        if k != 4:
            h, l = (1 - zh, lax.rem(zl + k, 4)) if k < 4 else (zh, lax.rem(zl + k - 4, 4))
            pl.semaphore_signal(barrier, inc=1, device_id=ring_device(h, l), device_id_type=MESH)
    others = [(q, t) for q in range(4) for t in range(4) if (q, t) != (0, 0)]
    for q, t in others:
        pl.semaphore_signal(barrier, inc=1, device_id=chip(q, t)[1], device_id_type=MESH)

    mine = g_ref.at[zh, s]
    contributions(counts_ref, values_ref, weights_ref, loads, mine, flip_ref)
    mine[64:65, :64] = (anchors_ref[0:1, :] - p * 8).astype(F32)
    mine[64:65, 64:] = anchors_ref[1:2, :].astype(F32)
    mine[65:66, :64] = anchors_ref[2:3, :].astype(F32)
    mine[65:66, 64:] = anchors_ref[2:3, :].astype(F32)
    pl.semaphore_wait(barrier, 23)

    def block(h, d):
        return g_ref.at[h, d, pl.ds(0, 66)]

    def hand(h, d, k):
        return remote(block(h, d), block(h, d), mate_send.at[k], mate_recv.at[k], mate)

    def source(k):
        same = k < 4
        h = jnp.where(same, zh, 1 - zh)
        return h, lax.rem(zl + 8 - k, 4) * 2 + c

    def arrive(k):
        h, d = source(k)
        remote(block(h, d), block(h, d), ring_send.at[k], ring_recv.at[k], mate).wait_recv()
        hand(h, d, k).start()

    def offer(k):
        h, l = (zh, lax.rem(zl + k, 4)) if k < 4 else (1 - zh, lax.rem(zl + k - 4, 4))
        return remote(
            block(zh, s), block(zh, s), ring_send.at[k], ring_recv.at[k], ring_device(h, l)
        )

    for k in (1, 3, 2):
        offer(k).start()
    hand(zh, s, 0).start()
    table = offset_table((32, 32), start, True)

    def turn_of(n):
        return jnp.where(n < 4, n, 4 + lax.rem(n + 1, 4))

    def gather_step(n, carry):
        @pl.when(jnp.logical_and(n > 0, n < 7))
        def _():
            arrive(turn_of(n + 1))

        k = turn_of(n)
        h, d = source(k)
        mate_d = d + 1 - 2 * c
        hand(h, mate_d, k).wait_recv()
        spread_pair((g_ref.at[h, d], g_ref.at[h, mate_d]), table, start, acc_ref)

        @pl.when(n == 0)
        def _():
            for k in (5, 7, 6, 4):
                offer(k).start()
            arrive(1)

        return carry

    sending = [(2, 2), (1, 2), (2, 1), (3, 2), (2, 3), (1, 1), (3, 3), (1, 3), (3, 1), (2, 0)]
    sending += [(0, 2), (1, 0), (0, 1), (3, 0), (0, 3)]

    def rows_of(ref, h, to):
        return ref.at[h, :, pl.ds(to * 16, 11)]

    def send_half(turn, h):
        for yy in range(11):
            for part in range(2):
                base = yy * 32 + part * 16
                for side in range(2):
                    field_ref[h, part * 2 + side, pl.ds(yy, 16, stride=16), :] = acc_ref[
                        base : base + 16, side * 128 : side * 128 + 128
                    ]
        copies = []
        for q, t in sending:
            to, device = chip(q, t)
            k = q * 4 + t
            copy = remote(
                rows_of(field_ref, h, to),
                rows_of(landed_ref, h, xy),
                to_send.at[turn, k],
                to_recv.at[turn, k],
                device,
            )
            copy.start()
            copies.append(copy)
        own = pltpu.make_async_copy(
            rows_of(field_ref, h, xy), rows_of(landed_ref, h, xy), local_sem.at[8 + turn]
        )
        own.start()
        return copies, own

    lax.fori_loop(0, 4, gather_step, 0)
    first_copies, first_own = send_half(0, zh)
    acc_ref[...] = jnp.zeros_like(acc_ref)
    lax.fori_loop(4, 8, gather_step, 0)
    second_copies, second_own = send_half(1, 1 - zh)
    for k in range(1, 8):
        offer(k).wait_send()
    for k in range(8):
        hand(0, 0, k).wait_send()
    for load in tables:
        load.wait()

    def landed(h):
        return right3(*halves(jnp.concatenate([landed_ref[h, k] for k in range(4)], axis=1)))

    first_own.wait()
    for copy in first_copies:
        copy.wait()
    fields = landed(zh)
    for n in range(4):
        along_ref[n] = mm(left3(yt_ref[0, zh, n], yt_ref[1, zh, n]), fields)
    second_own.wait()
    for copy in second_copies:
        copy.wait()
    fields = landed(1 - zh)
    z_table = zt_ref[...]
    highs, lows = [], []
    for n in range(4):
        u = along_ref[n] + mm(left3(yt_ref[0, 1 - zh, n], yt_ref[1, 1 - zh, n]), fields)
        real = u[:64, :N] + u[64:, N:]
        imag = u[:64, N:] - u[64:, :N]
        u = mm(left3(*halves(jnp.concatenate([real, imag], axis=0))), z_table)
        scale = spectrum_ref[0, n * 64 : n * 64 + 64] * (1.0 / (N * N * N))
        real = (u[:64, :N] + u[64:, N:]) * scale
        imag = (u[64:, :N] - u[:64, N:]) * scale
        u = mm(left3(*halves(jnp.concatenate([real, imag], axis=0))), z_table)
        real = u[:64, :N] - u[64:, N:]
        imag = u[64:, :N] + u[:64, N:]
        h, l = halves(jnp.concatenate([real, imag], axis=1))
        highs.append(h)
        lows.append(l)
    fields = right3(jnp.concatenate(highs, axis=0), jnp.concatenate(lows, axis=0))

    def return_half(turn, h):
        copies = []
        for q in (2, 1, 3, 0):
            column = lax.rem(gx + q, 4)
            u = mm(left3(yb_ref[0, h, column], yb_ref[1, h, column]), fields)
            real = u[:64, :N] - u[64:, N:]
            imag = u[:64, N:] + u[64:, :N]
            rows = pl.ds(column * 64, 64)
            smooth_ref[h, 0, rows] = real[:, :128]
            smooth_ref[h, 1, rows] = real[:, 128:]
            smooth_ref[h, 2, rows] = imag[:, :128]
            smooth_ref[h, 3, rows] = imag[:, 128:]
            for t in (1, 3, 2, 0):
                if (q, t) == (0, 0):
                    continue
                to, device = chip(q, t)
                k = q * 4 + t
                copy = remote(
                    rows_of(smooth_ref, h, to),
                    rows_of(back_ref, h, xy),
                    fro_send.at[turn, k],
                    fro_recv.at[turn, k],
                    device,
                )
                copy.start()
                copies.append(copy)
        own = pltpu.make_async_copy(
            rows_of(smooth_ref, h, xy), rows_of(back_ref, h, xy), local_sem.at[8 + turn]
        )
        own.start()
        return copies, own

    first_copies, first_own = return_half(0, 1 - zh)
    second_copies, second_own = return_half(1, zh)
    table = offset_table((8, 128), start, False)

    def member(k):
        other = k < 4
        h = jnp.where(other, 1 - zh, zh)
        return h, jnp.where(other, lax.rem(zl + k, 4), lax.rem(zl + k + 1, 4))

    def pass_on(k):
        return remote(mate_out.at[k], mate_in.at[k], mate2_send.at[k], mate2_recv.at[k], mate)

    def ring_on(k):
        h, l = member(k)
        return remote(
            own_sum.at[k], ring_in.at[k], ring2_send.at[k], ring2_recv.at[k], ring_device(h, l)
        )

    def pick_half(copies, own, h, base):
        own.wait()
        for copy in copies:
            copy.wait()
        for yy in range(11):
            for part in range(2):
                row = yy * 32 + part * 16
                for side in range(2):
                    piece = back_ref[h, part * 2 + side, pl.ds(yy, 16, stride=16), :]
                    first, second = halves(piece)
                    pair_ref[row : row + 16, side * 128 : side * 128 + 128] = first
                    pair_ref[row : row + 16, N + side * 128 : N + side * 128 + 128] = second

        def step(n, carry):
            k = base + n
            _, l = member(k)
            infos = (g_ref[h, l * 2 + 1 - c, 64:66], g_ref[h, l * 2 + c, 64:66])
            picked = pick_pair(infos, pair_ref[...], table, start)
            for i in range(4):
                mate_out[k, i * 8 : i * 8 + 8] = picked[:, i * 2 * N : i * 2 * N + N]
            pass_on(k).start()
            for i in range(4):
                own_sum[k, i * 8 : i * 8 + 8] = picked[:, i * 2 * N + N : (i + 1) * 2 * N]

            @pl.when(k > 0)
            def _():
                pass_on(k - 1).wait_recv()
                own_sum[k - 1] = own_sum[k - 1] + mate_in[k - 1]
                ring_on(k - 1).start()

            return carry

        lax.fori_loop(0, 4, step, 0)

    pick_half(first_copies, first_own, 1 - zh, 0)
    pick_half(second_copies, second_own, zh, 4)
    pass_on(7).wait_recv()
    total = own_sum[7] + mate_in[7]
    for k in range(7):
        ring_on(k).wait_recv()
        total = total + ring_in[k]
    results(counts_ref, total, weights_ref, out_ref, flip_ref)
    for k in range(8):
        pass_on(k).wait_send()
    for k in range(7):
        ring_on(k).wait_send()


def transform_tables():
    row = np.arange(512)
    h, xy, yy = row // 256, row // 16 % 16, row % 16
    used = (yy < 11).astype(np.float64)
    y = ((h * 16 + xy) * 8 - 1 + yy) % N
    k = np.arange(N)
    angle = 2 * np.pi * (k[:, None] * y[None, :] % N) / N
    cosine, sine = np.cos(angle) * used, np.sin(angle) * used
    forward = np.stack([cosine.reshape(4, 64, 2, N), sine.reshape(4, 64, 2, N)], axis=1)
    forward = forward.transpose(3, 0, 1, 2, 4).reshape(2, 4, 128, N)
    backward = np.stack([cosine.T.reshape(2, 4, 64, N), sine.T.reshape(2, 4, 64, N)], axis=2)
    backward = backward.reshape(2, 4, 128, N)
    angle = 2 * np.pi * (k[:, None] * k[None, :] % N) / N
    high, low = np_halves(np.concatenate([np.cos(angle), np.sin(angle)], axis=1))
    along = np.concatenate([high, low, high], axis=0)
    return np.stack(np_halves(forward)), along, np.stack(np_halves(backward))


def on_device(values, weights, anchors, counts, spectrum):
    dma = pltpu.SemaphoreType.DMA
    anywhere = pl.BlockSpec(memory_space=pl.ANY)
    tables = transform_tables()
    field = pltpu.VMEM((2, 4, 256, 128), F32)
    share = pltpu.VMEM((8, 32, N), F32)
    return pl.pallas_call(
        whole_kernel,
        out_shape=jax.ShapeDtypeStruct(values.shape, F32),
        in_specs=[SM, VM, VM] + [anywhere] * 5,
        out_specs=VM,
        scratch_shapes=[
            pltpu.VMEM(weights.shape, F32),
            pltpu.VMEM(spectrum.shape, F32),
            *[pltpu.VMEM(t.shape, BF16) for t in tables],
            pltpu.VMEM((128, 64), F32),
            pltpu.VMEM((2, 8, 72, 128), F32),
            pltpu.VMEM((352, N), F32),
            field,
            field,
            pltpu.VMEM((4, 128, 2 * N), F32),
            field,
            field,
            pltpu.VMEM((352, 2 * N), BF16),
            share,
            share,
            share,
            share,
            dma((10,)),
            *[dma((8,))] * 4,
            *[dma((2, 16))] * 4,
            *[dma((8,))] * 4,
        ],
        compiler_params=pltpu.CompilerParams(
            collective_id=1, has_side_effects=True, vmem_limit_bytes=LIMIT
        ),
    )(counts, values, anchors, weights, spectrum, *tables)


def solution(mesh):
    placed = (
        P(None, ("slab", "pencil")),
        P(("slab", "pencil"), None),
        P(None, ("slab", "pencil")),
        P(("slab", "pencil")),
        P(("slab", "pencil"), None, None),
    )
    return jax.shard_map(
        on_device,
        mesh=mesh,
        in_specs=placed,
        out_specs=P(None, ("slab", "pencil")),
        check_vma=False,
    )
```

```python
import math

import jax
import jax.numpy as jnp
import numpy as np
from jax import lax
from jax.experimental import pallas as pl
from jax.experimental.pallas import tpu as pltpu
from jax.sharding import PartitionSpec as P

MESH = pl.DeviceIdType.MESH
VM = pl.BlockSpec(memory_space=pltpu.VMEM)
SM = pl.BlockSpec(memory_space=pltpu.SMEM)
F32 = jnp.float32
BF16 = jnp.bfloat16
N = 256
LIMIT = 56 * 1024 * 1024


def halves(x):
    high = x.astype(BF16)
    low = (x - high.astype(F32)).astype(BF16)
    return high, low


def mm(a, b):
    return jnp.dot(a, b, preferred_element_type=F32)


def mm_nt(a, b):
    return lax.dot_general(a, b, (((1,), (1,)), ((), ())), preferred_element_type=F32)


def left3(high, low):
    return jnp.concatenate([high, high, low], axis=1)


def right3(high, low):
    return jnp.concatenate([high, low, high], axis=0)


def np_halves(x):
    x = np.asarray(x, np.float32)
    high = x.astype(jnp.bfloat16)
    low = (x - high.astype(np.float32)).astype(jnp.bfloat16)
    return high, low


def circle(m):
    x = (jnp.bitwise_and(m, N - 1) - N // 2).astype(F32) * (math.pi / N)
    y = x * x
    sine = jnp.full_like(x, -1.0 / 39916800)
    for f in (362880, -5040, 120, -6, 1):
        sine = sine * y + 1.0 / f
    sine = sine * x
    cosine = jnp.full_like(x, 1.0 / 479001600)
    for f in (-3628800, 40320, -720, 24, -2, 1):
        cosine = cosine * y + 1.0 / f
    return 2.0 * sine * sine - 1.0, -2.0 * sine * cosine


def remote(src, dst, send, recv, device):
    return pltpu.make_async_remote_copy(
        src_ref=src, dst_ref=dst, send_sem=send, recv_sem=recv, device_id=device, device_id_type=MESH
    )


def offset_table(shape, start, spread):
    at0 = lax.broadcasted_iota(jnp.int32, shape, 0)
    at1 = lax.broadcasted_iota(jnp.int32, shape, 1)
    if spread:
        group, span = at0, at1
        piece, span = span // 8, lax.rem(span, 8)
    else:
        group, span = lax.rem(at1, 32), at0
        piece = at1 // 32
    part, freq = group // 16, lax.rem(group, 16) + start
    r, offset = span // 4, lax.rem(span, 4) - 1
    cosine, sine = circle(freq * offset)
    exact = jnp.where(part == r, cosine, jnp.where(part == 0, sine, -sine))
    high = exact.astype(BF16).astype(F32)
    return jnp.where(piece < 2, high, exact - high).astype(BF16)


def phases(x_row, start):
    freq = lax.broadcasted_iota(jnp.int32, (16, x_row.shape[1]), 0) + start
    return circle(freq * x_row.astype(jnp.int32))


def z_hot(z_row):
    grid_z = lax.broadcasted_iota(jnp.int32, (N, z_row.shape[1]), 0)
    return (grid_z == z_row).astype(F32).astype(BF16)


def places(info):
    lane = lax.broadcasted_iota(jnp.int32, (8, 128), 1)
    first = lane < 64
    yz = jnp.broadcast_to(info[0:1], (8, 128))
    x = jnp.broadcast_to(info[1:2], (8, 128))
    zy = pltpu.roll(yz, 64, 1)
    y = jnp.where(first, yz, zy)
    z = jnp.where(first, zy, yz)
    x = jnp.where(first, x, pltpu.roll(x, 64, 1))
    y_row, z_row, x_row = (jnp.concatenate([v, v], axis=1)[0:1] for v in (y, z, x))
    j = lax.broadcasted_iota(jnp.int32, (1, N), 1) // 64
    z_row = jnp.bitwise_and(z_row.astype(jnp.int32) + (j - 1), N - 1)
    return y_row, z_row, x_row


def contributions(counts_ref, values_ref, weights_ref, waits, out_ref, flip_ref):
    for r in range(2):
        for b in range(64):
            flip_ref[r * 64 + b : r * 64 + b + 1, :] = values_ref[r : r + 1, b * 64 : b * 64 + 64]
    lane = lax.broadcasted_iota(jnp.int32, (64, 128), 1)
    first = lane < 64
    v = (flip_ref[:64, :], flip_ref[64:, :])
    totals = [jnp.zeros((64, 128), F32)] * 2
    for t in range(32):
        if t % 8 == 0:
            waits[t // 8].wait()
        tile = weights_ref[:, t * 128 : (t + 1) * 128]
        for r in range(2):
            spread = jnp.where(first, v[r][:, 2 * t : 2 * t + 1], v[r][:, 2 * t + 1 : 2 * t + 2])
            totals[r] = totals[r] + tile * spread
    totals = [t + pltpu.roll(t, 64, 1) for t in totals]
    both = jnp.where(first, totals[0], totals[1])
    row = lax.broadcasted_iota(jnp.int32, (64, 128), 0)
    both = jnp.where(row < counts_ref[0], both, 0.0)
    flipped = both.T
    for i in range(4):
        for j in range(4):
            for r in range(2):
                base = r * 64 + i * 16 + j * 4
                row = j // 2 * 32 + i * 8 + r * 4
                out_ref[row : row + 4, j % 2 * 64 : j % 2 * 64 + 64] = flipped[base : base + 4, :]


def results(counts_ref, picked, weights_ref, out_ref, flip_ref):
    for i in range(4):
        for j in range(4):
            for r in range(2):
                base = r * 64 + i * 16 + j * 4
                flip_ref[base : base + 4, :] = picked[i * 8 + r * 4 : i * 8 + r * 4 + 4, j * 64 : j * 64 + 64]
    both = flip_ref[...].T
    lane = lax.broadcasted_iota(jnp.int32, (64, 128), 1)
    first = lane < 64
    row = lax.broadcasted_iota(jnp.int32, (64, 128), 0)
    both = jnp.where(row < counts_ref[0], both, 0.0)
    turned = pltpu.roll(both, 64, 1)
    picks = (jnp.where(first, both, turned), jnp.where(first, turned, both))
    total = jnp.zeros((128, 64), F32)
    source = lax.broadcasted_iota(jnp.int32, (256, 64), 0) // 64
    target = lax.broadcasted_iota(jnp.int32, (256, 64), 1)
    for t in range(16):
        left = weights_ref[:, t * 256 : t * 256 + 128]
        right = weights_ref[:, t * 256 + 128 : t * 256 + 256]
        product = jnp.concatenate(
            [jnp.concatenate([left * pk, right * pk], axis=1) for pk in picks], axis=0
        )
        high, low = halves(product)
        collect = (target == source + 4 * t).astype(F32).astype(BF16)
        total = total + mm(high, collect) + mm(low, collect)
    for r in range(2):
        for b in range(64):
            out_ref[r : r + 1, b * 64 : b * 64 + 64] = total[r * 64 + b : r * 64 + b + 1, :]


def spread_pair(blocks, table, start, acc_ref):
    rows = [places(b[64:66]) for b in blocks]
    y_row, z_row, x_row = (jnp.concatenate([r[k] for r in rows], axis=1) for k in range(3))
    cosine, sine = phases(x_row, start)
    raw = jnp.concatenate(
        [
            b[k * 32 + i * 8 : k * 32 + i * 8 + 8]
            for i in range(4)
            for b in blocks
            for k in range(2)
        ],
        axis=1,
    )
    high = raw.astype(BF16).astype(F32)
    low = raw - high
    stacked = jnp.concatenate([high, low, high, low], axis=0).astype(BF16)
    flat = mm(table, stacked)
    parts = []
    for i in range(4):
        real = flat[:16, i * 2 * N : (i + 1) * 2 * N]
        imag = flat[16:, i * 2 * N : (i + 1) * 2 * N]
        parts.append(
            jnp.concatenate([cosine * real + sine * imag, cosine * imag - sine * real], axis=0)
        )
    y_all = jnp.broadcast_to(y_row, (32, 2 * N))
    pieces = []
    for yy in range(11):
        piece = jnp.zeros((32, 2 * N), F32)
        for i in range(4):
            if 0 <= yy - i < 8:
                piece = jnp.where(y_all == float(yy - i), parts[i], piece)
        pieces.append(jnp.concatenate(halves(piece), axis=1))
    hot = z_hot(z_row)
    acc_ref[...] += mm_nt(jnp.concatenate(pieces, axis=0), jnp.concatenate([hot, hot], axis=1))


def pick_pair(infos, smooth, table, start):
    rows = [places(info) for info in infos]
    y_row, z_row, x_row = (jnp.concatenate([r[k] for r in rows], axis=1) for k in range(3))
    cosine, sine = phases(x_row, start)
    hot = z_hot(z_row)
    rows = mm(smooth, jnp.concatenate([hot, hot], axis=0))
    y_all = jnp.broadcast_to(y_row, (32, 2 * N))
    turned = []
    for i in range(4):
        piece = rows[i * 32 : (i + 1) * 32]
        for y in range(1, 8):
            piece = jnp.where(y_all == float(y), rows[(y + i) * 32 : (y + i + 1) * 32], piece)
        real, imag = piece[:16], piece[16:]
        turned.append(
            jnp.concatenate([cosine * real - sine * imag, cosine * imag + sine * real], axis=0)
        )
    h, l = halves(jnp.concatenate(turned, axis=1))
    return mm(table, jnp.concatenate([h, l, h, l], axis=0))


def whole_kernel(
    counts_ref,
    values_ref,
    anchors_ref,
    weights_any,
    spectrum_any,
    yt_any,
    zt_any,
    yb_any,
    out_ref,
    weights_ref,
    spectrum_ref,
    yt_ref,
    zt_ref,
    yb_ref,
    flip_ref,
    g_ref,
    acc_ref,
    field_ref,
    landed_ref,
    along_ref,
    smooth_ref,
    back_ref,
    pair_ref,
    mate_out,
    mate_in,
    own_sum,
    ring_in,
    local_sem,
    ring_send,
    ring_recv,
    mate_send,
    mate_recv,
    to_send,
    to_recv,
    fro_send,
    fro_recv,
    ring2_send,
    ring2_recv,
    mate2_send,
    mate2_recv,
):
    s = lax.axis_index("slab")
    p = lax.axis_index("pencil")
    zl, c = s // 2, lax.rem(s, 2)
    zh, xy = p // 16, lax.rem(p, 16)
    gx, gy = xy // 4, lax.rem(xy, 4)
    start = s * 32 + zh * 16
    mate = (zl * 2 + 1 - c, p)

    def chip(q, t):
        to = lax.rem(gx + q, 4) * 4 + lax.rem(gy + t, 4)
        return to, (s, zh * 16 + to)

    def ring_device(h, l):
        return l * 2 + c, h * 16 + xy

    loads = []
    for k in range(4):
        cols = pl.ds(k * 1024, 1024)
        loads.append(
            pltpu.make_async_copy(weights_any.at[:, cols], weights_ref.at[:, cols], local_sem.at[k])
        )
    tables = [
        pltpu.make_async_copy(src, dst, local_sem.at[4 + k])
        for k, (src, dst) in enumerate(
            [
                (spectrum_any, spectrum_ref),
                (yt_any, yt_ref),
                (zt_any, zt_ref),
                (yb_any, yb_ref),
            ]
        )
    ]
    for load in loads + tables:
        load.start()
    landed_ref[...] = jnp.zeros_like(landed_ref)

    sending = [(2, 2), (1, 2), (2, 1), (3, 2), (2, 3), (1, 1), (3, 3), (1, 3), (3, 1), (2, 0)]
    sending += [(0, 2), (1, 0), (0, 1), (3, 0), (0, 3)]
    barrier = pltpu.get_barrier_semaphore()

    def greet(device):
        pl.semaphore_signal(barrier, inc=1, device_id=device, device_id_type=MESH)

    for k in (0, 1, 3, 2):
        greet(ring_device(1 - zh, lax.rem(zl + k, 4)))
    for q, t in sending:
        greet(chip(q, t)[1])
    for k in (1, 3, 2):
        greet(ring_device(zh, lax.rem(zl + k, 4)))
    greet(mate)
    acc_ref[...] = jnp.zeros_like(acc_ref)

    mine = g_ref.at[zh, s]
    contributions(counts_ref, values_ref, weights_ref, loads, mine, flip_ref)
    mine[64:65, :64] = (anchors_ref[0:1, :] - p * 8).astype(F32)
    mine[64:65, 64:] = anchors_ref[1:2, :].astype(F32)
    mine[65:66, :64] = anchors_ref[2:3, :].astype(F32)
    mine[65:66, 64:] = anchors_ref[2:3, :].astype(F32)
    pl.semaphore_wait(barrier, 23)

    def block(h, d):
        return g_ref.at[h, d, pl.ds(0, 66)]

    def hand(h, d, k):
        return remote(block(h, d), block(h, d), mate_send.at[k], mate_recv.at[k], mate)

    def source(k):
        same = k < 4
        h = jnp.where(same, zh, 1 - zh)
        return h, lax.rem(zl + 8 - k, 4) * 2 + c

    z = zh * 4 + zl

    def along_ring(t):
        to = lax.rem(z + 8 + t, 8)
        return ring_device(to // 4, lax.rem(to, 4))

    def place_of(t):
        at = lax.rem(z + 8 + t, 8)
        return block(at // 4, lax.rem(at, 4) * 2 + c)

    def step_on(t, u, k):
        slot = lax.rem(u - t + 8, 8)
        return remote(
            place_of(t), place_of(t), ring_send.at[k], ring_recv.at[slot], along_ring(u)
        )

    def landed_from(t):
        slot = lax.rem(8 - t, 8)
        return remote(place_of(t), place_of(t), ring_send.at[0], ring_recv.at[slot], mate)

    way = 1 - 2 * lax.rem(z, 2)
    direct = [step_on(0, u, k) for k, u in enumerate((2, -2, 1, -1))]
    relays = [step_on(-2, 1, 4), step_on(2, -1, 5), step_on(-2 * way, 2 * way, 6)]

    def arrive(k):
        h, d = source(k)
        back = lax.rem(z - h * 4 - d // 2 + 8, 8)

        @pl.when(jnp.logical_and(back != 2, back != 6))
        def _():
            place = block(h, d)
            remote(place, place, ring_send.at[0], ring_recv.at[back], mate).wait_recv()

        hand(h, d, k).start()

    for copy in direct:
        copy.start()
    hand(zh, s, 0).start()
    table = offset_table((32, 32), start, True)

    def turn_of(n):
        return jnp.where(n < 4, n, 4 + lax.rem(n + 1, 4))

    def gather_step(n, carry):
        @pl.when(jnp.logical_and(n > 0, n < 7))
        def _():
            arrive(turn_of(n + 1))

        k = turn_of(n)
        h, d = source(k)
        mate_d = d + 1 - 2 * c
        hand(h, mate_d, k).wait_recv()
        spread_pair((g_ref.at[h, d], g_ref.at[h, mate_d]), table, start, acc_ref)

        @pl.when(n == 0)
        def _():
            landed_from(-2).wait_recv()
            landed_from(2).wait_recv()
            for copy in relays:
                copy.start()
            arrive(1)

        return carry

    def rows_of(ref, h, to):
        return ref.at[h, :, pl.ds(to * 16, 11)]

    def send_half(turn, h):
        for yy in range(11):
            for part in range(2):
                base = yy * 32 + part * 16
                for side in range(2):
                    field_ref[h, part * 2 + side, pl.ds(yy, 16, stride=16), :] = acc_ref[
                        base : base + 16, side * 128 : side * 128 + 128
                    ]
        copies = []
        for q, t in sending:
            to, device = chip(q, t)
            k = q * 4 + t
            copy = remote(
                rows_of(field_ref, h, to),
                rows_of(landed_ref, h, xy),
                to_send.at[turn, k],
                to_recv.at[turn, k],
                device,
            )
            copy.start()
            copies.append(copy)
        own = pltpu.make_async_copy(
            rows_of(field_ref, h, xy), rows_of(landed_ref, h, xy), local_sem.at[8 + turn]
        )
        own.start()
        return copies, own

    lax.fori_loop(0, 4, gather_step, 0)
    first_copies, first_own = send_half(0, zh)
    acc_ref[...] = jnp.zeros_like(acc_ref)
    lax.fori_loop(4, 8, gather_step, 0)
    second_copies, second_own = send_half(1, 1 - zh)
    for load in tables:
        load.wait()

    def landed(h):
        return right3(*halves(jnp.concatenate([landed_ref[h, k] for k in range(4)], axis=1)))

    first_own.wait()
    for copy in first_copies:
        copy.wait_recv()
    fields = landed(zh)
    for n in range(4):
        along_ref[n] = mm(left3(yt_ref[0, zh, n], yt_ref[1, zh, n]), fields)
    second_own.wait()
    for copy in second_copies:
        copy.wait_recv()
    fields = landed(1 - zh)
    z_table = zt_ref[...]
    highs, lows = [], []
    for n in range(4):
        u = along_ref[n] + mm(left3(yt_ref[0, 1 - zh, n], yt_ref[1, 1 - zh, n]), fields)
        real = u[:64, :N] + u[64:, N:]
        imag = u[:64, N:] - u[64:, :N]
        u = mm(left3(*halves(jnp.concatenate([real, imag], axis=0))), z_table)
        scale = spectrum_ref[0, n * 64 : n * 64 + 64] * (1.0 / (N * N * N))
        real = (u[:64, :N] + u[64:, N:]) * scale
        imag = (u[64:, :N] - u[:64, N:]) * scale
        u = mm(left3(*halves(jnp.concatenate([real, imag], axis=0))), z_table)
        real = u[:64, :N] - u[64:, N:]
        imag = u[64:, :N] + u[:64, N:]
        h, l = halves(jnp.concatenate([real, imag], axis=1))
        highs.append(h)
        lows.append(l)
    fields = right3(jnp.concatenate(highs, axis=0), jnp.concatenate(lows, axis=0))

    def return_half(turn, h):
        copies = []
        for q in (2, 1, 3, 0):
            column = lax.rem(gx + q, 4)
            u = mm(left3(yb_ref[0, h, column], yb_ref[1, h, column]), fields)
            real = u[:64, :N] - u[64:, N:]
            imag = u[:64, N:] + u[64:, :N]
            rows = pl.ds(column * 64, 64)
            smooth_ref[h, 0, rows] = real[:, :128]
            smooth_ref[h, 1, rows] = real[:, 128:]
            smooth_ref[h, 2, rows] = imag[:, :128]
            smooth_ref[h, 3, rows] = imag[:, 128:]
            for t in (1, 3, 2, 0):
                if (q, t) == (0, 0):
                    continue
                to, device = chip(q, t)
                k = q * 4 + t
                copy = remote(
                    rows_of(smooth_ref, h, to),
                    rows_of(back_ref, h, xy),
                    fro_send.at[turn, k],
                    fro_recv.at[turn, k],
                    device,
                )
                copy.start()
                copies.append(copy)
        own = pltpu.make_async_copy(
            rows_of(smooth_ref, h, xy), rows_of(back_ref, h, xy), local_sem.at[8 + turn]
        )
        own.start()
        return copies, own

    sent = first_copies + second_copies
    first_copies, first_own = return_half(0, 1 - zh)
    second_copies, second_own = return_half(1, zh)
    sent = sent + first_copies + second_copies
    table = offset_table((8, 128), start, False)

    def member(k):
        other = k < 4
        h = jnp.where(other, 1 - zh, zh)
        return h, jnp.where(other, lax.rem(zl + k, 4), lax.rem(zl + k + 1, 4))

    def pass_on(k):
        return remote(mate_out.at[k], mate_in.at[k], mate2_send.at[k], mate2_recv.at[k], mate)

    def ring_on(k):
        h, l = member(k)
        return remote(
            own_sum.at[k], ring_in.at[k], ring2_send.at[k], ring2_recv.at[k], ring_device(h, l)
        )

    def pick_half(copies, own, h, base):
        own.wait()
        for copy in copies:
            copy.wait_recv()
        for yy in range(11):
            for part in range(2):
                row = yy * 32 + part * 16
                for side in range(2):
                    piece = back_ref[h, part * 2 + side, pl.ds(yy, 16, stride=16), :]
                    first, second = halves(piece)
                    pair_ref[row : row + 16, side * 128 : side * 128 + 128] = first
                    pair_ref[row : row + 16, N + side * 128 : N + side * 128 + 128] = second

        def step(n, carry):
            k = base + n
            _, l = member(k)
            infos = (g_ref[h, l * 2 + 1 - c, 64:66], g_ref[h, l * 2 + c, 64:66])
            picked = pick_pair(infos, pair_ref[...], table, start)
            for i in range(4):
                mate_out[k, i * 8 : i * 8 + 8] = picked[:, i * 2 * N : i * 2 * N + N]
            pass_on(k).start()
            for i in range(4):
                own_sum[k, i * 8 : i * 8 + 8] = picked[:, i * 2 * N + N : (i + 1) * 2 * N]

            @pl.when(k > 0)
            def _():
                pass_on(k - 1).wait_recv()
                own_sum[k - 1] = own_sum[k - 1] + mate_in[k - 1]
                ring_on(k - 1).start()

            return carry

        lax.fori_loop(0, 4, step, 0)

    pick_half(first_copies, first_own, 1 - zh, 0)
    pick_half(second_copies, second_own, zh, 4)
    pass_on(7).wait_recv()
    total = own_sum[7] + mate_in[7]
    for k in range(7):
        ring_on(k).wait_recv()
        total = total + ring_in[k]
    results(counts_ref, total, weights_ref, out_ref, flip_ref)
    for copy in direct + relays + sent:
        copy.wait_send()
    for k in range(8):
        hand(0, 0, k).wait_send()
        pass_on(k).wait_send()
    for k in range(7):
        ring_on(k).wait_send()


def transform_tables():
    row = np.arange(512)
    h, xy, yy = row // 256, row // 16 % 16, row % 16
    used = (yy < 11).astype(np.float64)
    y = ((h * 16 + xy) * 8 - 1 + yy) % N
    k = np.arange(N)
    angle = 2 * np.pi * (k[:, None] * y[None, :] % N) / N
    cosine, sine = np.cos(angle) * used, np.sin(angle) * used
    forward = np.stack([cosine.reshape(4, 64, 2, N), sine.reshape(4, 64, 2, N)], axis=1)
    forward = forward.transpose(3, 0, 1, 2, 4).reshape(2, 4, 128, N)
    backward = np.stack([cosine.T.reshape(2, 4, 64, N), sine.T.reshape(2, 4, 64, N)], axis=2)
    backward = backward.reshape(2, 4, 128, N)
    angle = 2 * np.pi * (k[:, None] * k[None, :] % N) / N
    high, low = np_halves(np.concatenate([np.cos(angle), np.sin(angle)], axis=1))
    along = np.concatenate([high, low, high], axis=0)
    return np.stack(np_halves(forward)), along, np.stack(np_halves(backward))


def on_device(values, weights, anchors, counts, spectrum):
    dma = pltpu.SemaphoreType.DMA
    anywhere = pl.BlockSpec(memory_space=pl.ANY)
    tables = transform_tables()
    field = pltpu.VMEM((2, 4, 256, 128), F32)
    strided = pltpu.VMEM((2, 4, 272, 128), F32)
    share = pltpu.VMEM((8, 32, N), F32)
    return pl.pallas_call(
        whole_kernel,
        out_shape=jax.ShapeDtypeStruct(values.shape, F32),
        in_specs=[SM, VM, VM] + [anywhere] * 5,
        out_specs=VM,
        scratch_shapes=[
            pltpu.VMEM(weights.shape, F32),
            pltpu.VMEM(spectrum.shape, F32),
            *[pltpu.VMEM(t.shape, BF16) for t in tables],
            pltpu.VMEM((128, 64), F32),
            pltpu.VMEM((2, 8, 72, 128), F32),
            pltpu.VMEM((352, N), F32),
            strided,
            field,
            pltpu.VMEM((4, 128, 2 * N), F32),
            field,
            strided,
            pltpu.VMEM((352, 2 * N), BF16),
            share,
            share,
            share,
            share,
            dma((10,)),
            *[dma((8,))] * 4,
            *[dma((2, 16))] * 4,
            *[dma((8,))] * 4,
        ],
        compiler_params=pltpu.CompilerParams(
            collective_id=1, has_side_effects=True, vmem_limit_bytes=LIMIT
        ),
    )(counts, values, anchors, weights, spectrum, *tables)


def solution(mesh):
    placed = (
        P(None, ("slab", "pencil")),
        P(("slab", "pencil"), None),
        P(None, ("slab", "pencil")),
        P(("slab", "pencil")),
        P(("slab", "pencil"), None, None),
    )
    return jax.shard_map(
        on_device,
        mesh=mesh,
        in_specs=placed,
        out_specs=P(None, ("slab", "pencil")),
        check_vma=False,
    )
```

```python
import math

import jax
import jax.numpy as jnp
import numpy as np
from jax import lax
from jax.experimental import pallas as pl
from jax.experimental.pallas import tpu as pltpu
from jax.sharding import PartitionSpec as P

MESH = pl.DeviceIdType.MESH
VM = pl.BlockSpec(memory_space=pltpu.VMEM)
SM = pl.BlockSpec(memory_space=pltpu.SMEM)
F32 = jnp.float32
BF16 = jnp.bfloat16
N = 256
LIMIT = 56 * 1024 * 1024


def halves(x):
    high = x.astype(BF16)
    low = (x - high.astype(F32)).astype(BF16)
    return high, low


def mm(a, b):
    return jnp.dot(a, b, preferred_element_type=F32)


def mm_nt(a, b):
    return lax.dot_general(a, b, (((1,), (1,)), ((), ())), preferred_element_type=F32)


def left3(high, low):
    return jnp.concatenate([high, high, low], axis=1)


def right3(high, low):
    return jnp.concatenate([high, low, high], axis=0)


def np_halves(x):
    x = np.asarray(x, np.float32)
    high = x.astype(jnp.bfloat16)
    low = (x - high.astype(np.float32)).astype(jnp.bfloat16)
    return high, low


def circle(m):
    x = (jnp.bitwise_and(m, N - 1) - N // 2).astype(F32) * (math.pi / N)
    y = x * x
    sine = jnp.full_like(x, -1.0 / 39916800)
    for f in (362880, -5040, 120, -6, 1):
        sine = sine * y + 1.0 / f
    sine = sine * x
    cosine = jnp.full_like(x, 1.0 / 479001600)
    for f in (-3628800, 40320, -720, 24, -2, 1):
        cosine = cosine * y + 1.0 / f
    return 2.0 * sine * sine - 1.0, -2.0 * sine * cosine


def remote(src, dst, send, recv, device):
    return pltpu.make_async_remote_copy(
        src_ref=src, dst_ref=dst, send_sem=send, recv_sem=recv, device_id=device, device_id_type=MESH
    )


def offset_table(shape, start, spread):
    at0 = lax.broadcasted_iota(jnp.int32, shape, 0)
    at1 = lax.broadcasted_iota(jnp.int32, shape, 1)
    if spread:
        group, span = at0, at1
        piece, span = span // 8, lax.rem(span, 8)
    else:
        group, span = lax.rem(at1, 32), at0
        piece = at1 // 32
    part, freq = group // 16, lax.rem(group, 16) + start
    r, offset = span // 4, lax.rem(span, 4) - 1
    cosine, sine = circle(freq * offset)
    exact = jnp.where(part == r, cosine, jnp.where(part == 0, sine, -sine))
    high = exact.astype(BF16).astype(F32)
    return jnp.where(piece < 2, high, exact - high).astype(BF16)


def phases(x_row, start):
    freq = lax.broadcasted_iota(jnp.int32, (16, x_row.shape[1]), 0) + start
    return circle(freq * x_row.astype(jnp.int32))


def z_hot(z_row):
    grid_z = lax.broadcasted_iota(jnp.int32, (N, z_row.shape[1]), 0)
    return (grid_z == z_row).astype(F32).astype(BF16)


def places(info):
    lane = lax.broadcasted_iota(jnp.int32, (8, 128), 1)
    first = lane < 64
    yz = jnp.broadcast_to(info[0:1], (8, 128))
    x = jnp.broadcast_to(info[1:2], (8, 128))
    zy = pltpu.roll(yz, 64, 1)
    y = jnp.where(first, yz, zy)
    z = jnp.where(first, zy, yz)
    x = jnp.where(first, x, pltpu.roll(x, 64, 1))
    y_row, z_row, x_row = (jnp.concatenate([v, v], axis=1)[0:1] for v in (y, z, x))
    j = lax.broadcasted_iota(jnp.int32, (1, N), 1) // 64
    z_row = jnp.bitwise_and(z_row.astype(jnp.int32) + (j - 1), N - 1)
    return y_row, z_row, x_row


def contributions(counts_ref, values_ref, weights_ref, waits, out_ref, flip_ref):
    for r in range(2):
        for b in range(64):
            flip_ref[r * 64 + b : r * 64 + b + 1, :] = values_ref[r : r + 1, b * 64 : b * 64 + 64]
    lane = lax.broadcasted_iota(jnp.int32, (64, 128), 1)
    first = lane < 64
    v = (flip_ref[:64, :], flip_ref[64:, :])
    totals = [jnp.zeros((64, 128), F32)] * 2
    for t in range(32):
        if t % 8 == 0:
            waits[t // 8].wait()
        tile = weights_ref[:, t * 128 : (t + 1) * 128]
        for r in range(2):
            spread = jnp.where(first, v[r][:, 2 * t : 2 * t + 1], v[r][:, 2 * t + 1 : 2 * t + 2])
            totals[r] = totals[r] + tile * spread
    totals = [t + pltpu.roll(t, 64, 1) for t in totals]
    both = jnp.where(first, totals[0], totals[1])
    row = lax.broadcasted_iota(jnp.int32, (64, 128), 0)
    both = jnp.where(row < counts_ref[0], both, 0.0)
    flipped = both.T
    for i in range(4):
        for j in range(4):
            for r in range(2):
                base = r * 64 + i * 16 + j * 4
                row = j // 2 * 32 + i * 8 + r * 4
                out_ref[row : row + 4, j % 2 * 64 : j % 2 * 64 + 64] = flipped[base : base + 4, :]


def results(counts_ref, picked, weights_ref, out_ref, flip_ref):
    for i in range(4):
        for j in range(4):
            for r in range(2):
                base = r * 64 + i * 16 + j * 4
                flip_ref[base : base + 4, :] = picked[i * 8 + r * 4 : i * 8 + r * 4 + 4, j * 64 : j * 64 + 64]
    both = flip_ref[...].T
    lane = lax.broadcasted_iota(jnp.int32, (64, 128), 1)
    first = lane < 64
    row = lax.broadcasted_iota(jnp.int32, (64, 128), 0)
    both = jnp.where(row < counts_ref[0], both, 0.0)
    turned = pltpu.roll(both, 64, 1)
    picks = (jnp.where(first, both, turned), jnp.where(first, turned, both))
    total = jnp.zeros((128, 64), F32)
    source = lax.broadcasted_iota(jnp.int32, (256, 64), 0) // 64
    target = lax.broadcasted_iota(jnp.int32, (256, 64), 1)
    for t in range(16):
        left = weights_ref[:, t * 256 : t * 256 + 128]
        right = weights_ref[:, t * 256 + 128 : t * 256 + 256]
        product = jnp.concatenate(
            [jnp.concatenate([left * pk, right * pk], axis=1) for pk in picks], axis=0
        )
        high, low = halves(product)
        collect = (target == source + 4 * t).astype(F32).astype(BF16)
        total = total + mm(high, collect) + mm(low, collect)
    for r in range(2):
        for b in range(64):
            out_ref[r : r + 1, b * 64 : b * 64 + 64] = total[r * 64 + b : r * 64 + b + 1, :]


def spread_pair(blocks, table, start, acc_ref):
    rows = [places(b[64:66]) for b in blocks]
    y_row, z_row, x_row = (jnp.concatenate([r[k] for r in rows], axis=1) for k in range(3))
    cosine, sine = phases(x_row, start)
    raw = jnp.concatenate(
        [
            b[k * 32 + i * 8 : k * 32 + i * 8 + 8]
            for i in range(4)
            for b in blocks
            for k in range(2)
        ],
        axis=1,
    )
    high = raw.astype(BF16).astype(F32)
    low = raw - high
    stacked = jnp.concatenate([high, low, high, low], axis=0).astype(BF16)
    flat = mm(table, stacked)
    parts = []
    for i in range(4):
        real = flat[:16, i * 2 * N : (i + 1) * 2 * N]
        imag = flat[16:, i * 2 * N : (i + 1) * 2 * N]
        parts.append(
            jnp.concatenate([cosine * real + sine * imag, cosine * imag - sine * real], axis=0)
        )
    y_all = jnp.broadcast_to(y_row, (32, 2 * N))
    pieces = []
    for yy in range(11):
        piece = jnp.zeros((32, 2 * N), F32)
        for i in range(4):
            if 0 <= yy - i < 8:
                piece = jnp.where(y_all == float(yy - i), parts[i], piece)
        pieces.append(jnp.concatenate(halves(piece), axis=1))
    hot = z_hot(z_row)
    acc_ref[...] += mm_nt(jnp.concatenate(pieces, axis=0), jnp.concatenate([hot, hot], axis=1))


def pick_pair(infos, smooth, table, start):
    rows = [places(info) for info in infos]
    y_row, z_row, x_row = (jnp.concatenate([r[k] for r in rows], axis=1) for k in range(3))
    cosine, sine = phases(x_row, start)
    hot = z_hot(z_row)
    rows = mm(smooth, jnp.concatenate([hot, hot], axis=0))
    y_all = jnp.broadcast_to(y_row, (32, 2 * N))
    turned = []
    for i in range(4):
        piece = rows[i * 32 : (i + 1) * 32]
        for y in range(1, 8):
            piece = jnp.where(y_all == float(y), rows[(y + i) * 32 : (y + i + 1) * 32], piece)
        real, imag = piece[:16], piece[16:]
        turned.append(
            jnp.concatenate([cosine * real - sine * imag, cosine * imag + sine * real], axis=0)
        )
    h, l = halves(jnp.concatenate(turned, axis=1))
    return mm(table, jnp.concatenate([h, l, h, l], axis=0))


def whole_kernel(
    counts_ref,
    values_ref,
    anchors_ref,
    weights_any,
    spectrum_any,
    yt_any,
    zt_any,
    yb_any,
    out_ref,
    weights_ref,
    spectrum_ref,
    yt_ref,
    zt_ref,
    yb_ref,
    flip_ref,
    g_ref,
    acc_ref,
    field_ref,
    landed_ref,
    along_ref,
    smooth_ref,
    back_ref,
    pair_ref,
    mate_out,
    mate_in,
    own_sum,
    ring_in,
    local_sem,
    ring_send,
    ring_recv,
    mate_send,
    mate_recv,
    to_send,
    to_recv,
    fro_send,
    fro_recv,
    ring2_send,
    ring2_recv,
    mate2_send,
    mate2_recv,
):
    s = lax.axis_index("slab")
    p = lax.axis_index("pencil")
    zl, c = s // 2, lax.rem(s, 2)
    zh, xy = p // 16, lax.rem(p, 16)
    gx, gy = xy // 4, lax.rem(xy, 4)
    start = s * 32 + zh * 16
    mate = (zl * 2 + 1 - c, p)

    def chip(q, t):
        to = lax.rem(gx + q, 4) * 4 + lax.rem(gy + t, 4)
        return to, (s, zh * 16 + to)

    def ring_device(h, l):
        return l * 2 + c, h * 16 + xy

    loads = []
    for k in range(4):
        cols = pl.ds(k * 1024, 1024)
        loads.append(
            pltpu.make_async_copy(weights_any.at[:, cols], weights_ref.at[:, cols], local_sem.at[k])
        )
    tables = [
        pltpu.make_async_copy(src, dst, local_sem.at[4 + k])
        for k, (src, dst) in enumerate(
            [
                (spectrum_any, spectrum_ref),
                (yt_any, yt_ref),
                (zt_any, zt_ref),
                (yb_any, yb_ref),
            ]
        )
    ]
    for load in loads + tables:
        load.start()
    landed_ref[...] = jnp.zeros_like(landed_ref)

    sending = [(2, 2), (1, 2), (2, 1), (3, 2), (2, 3), (1, 1), (3, 3), (1, 3), (3, 1), (2, 0)]
    sending += [(0, 2), (1, 0), (0, 1), (3, 0), (0, 3)]
    barrier = pltpu.get_barrier_semaphore()

    def greet(device):
        pl.semaphore_signal(barrier, inc=1, device_id=device, device_id_type=MESH)

    for k in (0, 1, 3, 2):
        greet(ring_device(1 - zh, lax.rem(zl + k, 4)))
    for q, t in sending:
        greet(chip(q, t)[1])
    for k in (1, 3, 2):
        greet(ring_device(zh, lax.rem(zl + k, 4)))
    greet(mate)
    acc_ref[...] = jnp.zeros_like(acc_ref)

    mine = g_ref.at[zh, s]
    contributions(counts_ref, values_ref, weights_ref, loads, mine, flip_ref)
    mine[64:65, :64] = (anchors_ref[0:1, :] - p * 8).astype(F32)
    mine[64:65, 64:] = anchors_ref[1:2, :].astype(F32)
    mine[65:66, :64] = anchors_ref[2:3, :].astype(F32)
    mine[65:66, 64:] = anchors_ref[2:3, :].astype(F32)
    pl.semaphore_wait(barrier, 23)

    def block(h, d):
        return g_ref.at[h, d, pl.ds(0, 66)]

    def hand(h, d, k):
        return remote(block(h, d), block(h, d), mate_send.at[k], mate_recv.at[k], mate)

    def source(k):
        same = k < 4
        h = jnp.where(same, zh, 1 - zh)
        return h, lax.rem(zl + 8 - k, 4) * 2 + c

    z = zh * 4 + zl

    def along_ring(t):
        to = lax.rem(z + 8 + t, 8)
        return ring_device(to // 4, lax.rem(to, 4))

    def place_of(t):
        at = lax.rem(z + 8 + t, 8)
        return block(at // 4, lax.rem(at, 4) * 2 + c)

    def step_on(t, u, k):
        slot = lax.rem(u - t + 8, 8)
        return remote(
            place_of(t), place_of(t), ring_send.at[k], ring_recv.at[slot], along_ring(u)
        )

    def landed_from(t):
        slot = lax.rem(8 - t, 8)
        return remote(place_of(t), place_of(t), ring_send.at[0], ring_recv.at[slot], mate)

    way = 1 - 2 * lax.rem(z, 2)
    direct = [step_on(0, u, k) for k, u in enumerate((2, -2, 1, -1))]
    relays = [step_on(-2, 1, 4), step_on(2, -1, 5), step_on(-2 * way, 2 * way, 6)]

    def arrive(k):
        h, d = source(k)
        back = lax.rem(z - h * 4 - d // 2 + 8, 8)

        @pl.when(jnp.logical_and(back != 2, back != 6))
        def _():
            place = block(h, d)
            remote(place, place, ring_send.at[0], ring_recv.at[back], mate).wait_recv()

        hand(h, d, k).start()

    for copy in direct:
        copy.start()
    hand(zh, s, 0).start()
    table = offset_table((32, 32), start, True)

    def turn_of(n):
        m = lax.rem(n, 4)
        inner = jnp.where(m >= 2, 5 - m, m)
        own_half = jnp.where(zl == 3, m, jnp.where(zl == 0, lax.rem(4 - m, 4), inner))
        inner = jnp.where(m == 2, 7, jnp.where(m == 3, 4, 6 - m))
        other = jnp.where(zl == 3, 7 - m, jnp.where(zl == 0, 4 + lax.rem(m + 1, 4), inner))
        return jnp.where(n < 4, own_half, other)

    def gather_step(n, carry):
        @pl.when(jnp.logical_and(n != 3, n < 7))
        def _():
            arrive(turn_of(n + 1))

        k = turn_of(n)
        h, d = source(k)
        mate_d = d + 1 - 2 * c
        hand(h, mate_d, k).wait_recv()
        spread_pair((g_ref.at[h, d], g_ref.at[h, mate_d]), table, start, acc_ref)

        @pl.when(n == 0)
        def _():
            landed_from(-2).wait_recv()
            landed_from(2).wait_recv()
            for copy in relays:
                copy.start()

        return carry

    def rows_of(ref, h, to):
        return ref.at[h, :, pl.ds(to * 16, 11)]

    def send_half(turn, h):
        for yy in range(11):
            for part in range(2):
                base = yy * 32 + part * 16
                for side in range(2):
                    field_ref[h, part * 2 + side, pl.ds(yy, 16, stride=16), :] = acc_ref[
                        base : base + 16, side * 128 : side * 128 + 128
                    ]
        copies = []
        for q, t in sending:
            to, device = chip(q, t)
            k = q * 4 + t
            copy = remote(
                rows_of(field_ref, h, to),
                rows_of(landed_ref, h, xy),
                to_send.at[turn, k],
                to_recv.at[turn, k],
                device,
            )
            copy.start()
            copies.append(copy)
        own = pltpu.make_async_copy(
            rows_of(field_ref, h, xy), rows_of(landed_ref, h, xy), local_sem.at[8 + turn]
        )
        own.start()
        return copies, own

    lax.fori_loop(0, 4, gather_step, 0)
    first_copies, first_own = send_half(0, zh)
    acc_ref[...] = jnp.zeros_like(acc_ref)
    arrive(turn_of(4))
    lax.fori_loop(4, 8, gather_step, 0)
    second_copies, second_own = send_half(1, 1 - zh)
    for load in tables:
        load.wait()

    def landed(h):
        return right3(*halves(jnp.concatenate([landed_ref[h, k] for k in range(4)], axis=1)))

    first_own.wait()
    for copy in first_copies:
        copy.wait_recv()
    fields = landed(zh)
    for n in range(4):
        along_ref[n] = mm(left3(yt_ref[0, zh, n], yt_ref[1, zh, n]), fields)
    second_own.wait()
    for copy in second_copies:
        copy.wait_recv()
    fields = landed(1 - zh)
    z_table = zt_ref[...]
    highs, lows = [], []
    for n in range(4):
        u = along_ref[n] + mm(left3(yt_ref[0, 1 - zh, n], yt_ref[1, 1 - zh, n]), fields)
        real = u[:64, :N] + u[64:, N:]
        imag = u[:64, N:] - u[64:, :N]
        u = mm(left3(*halves(jnp.concatenate([real, imag], axis=0))), z_table)
        scale = spectrum_ref[0, n * 64 : n * 64 + 64] * (1.0 / (N * N * N))
        real = (u[:64, :N] + u[64:, N:]) * scale
        imag = (u[64:, :N] - u[:64, N:]) * scale
        u = mm(left3(*halves(jnp.concatenate([real, imag], axis=0))), z_table)
        real = u[:64, :N] - u[64:, N:]
        imag = u[64:, :N] + u[:64, N:]
        h, l = halves(jnp.concatenate([real, imag], axis=1))
        highs.append(h)
        lows.append(l)
    fields = right3(jnp.concatenate(highs, axis=0), jnp.concatenate(lows, axis=0))

    def return_half(turn, h):
        copies = []
        for q in (2, 1, 3, 0):
            column = lax.rem(gx + q, 4)
            u = mm(left3(yb_ref[0, h, column], yb_ref[1, h, column]), fields)
            real = u[:64, :N] - u[64:, N:]
            imag = u[:64, N:] + u[64:, :N]
            rows = pl.ds(column * 64, 64)
            smooth_ref[h, 0, rows] = real[:, :128]
            smooth_ref[h, 1, rows] = real[:, 128:]
            smooth_ref[h, 2, rows] = imag[:, :128]
            smooth_ref[h, 3, rows] = imag[:, 128:]
            for t in (1, 3, 2, 0):
                if (q, t) == (0, 0):
                    continue
                to, device = chip(q, t)
                k = q * 4 + t
                copy = remote(
                    rows_of(smooth_ref, h, to),
                    rows_of(back_ref, h, xy),
                    fro_send.at[turn, k],
                    fro_recv.at[turn, k],
                    device,
                )
                copy.start()
                copies.append(copy)
        own = pltpu.make_async_copy(
            rows_of(smooth_ref, h, xy), rows_of(back_ref, h, xy), local_sem.at[8 + turn]
        )
        own.start()
        return copies, own

    sent = first_copies + second_copies
    first_copies, first_own = return_half(0, 1 - zh)
    second_copies, second_own = return_half(1, zh)
    sent = sent + first_copies + second_copies
    table = offset_table((8, 128), start, False)

    def member(k):
        other = k < 4
        h = jnp.where(other, 1 - zh, zh)
        return h, jnp.where(other, lax.rem(zl + k, 4), lax.rem(zl + k + 1, 4))

    def pass_on(k):
        return remote(mate_out.at[k], mate_in.at[k], mate2_send.at[k], mate2_recv.at[k], mate)

    def ring_on(k):
        h, l = member(k)
        return remote(
            own_sum.at[k], ring_in.at[k], ring2_send.at[k], ring2_recv.at[k], ring_device(h, l)
        )

    def pick_half(copies, own, h, base):
        own.wait()
        for copy in copies:
            copy.wait_recv()
        for yy in range(11):
            for part in range(2):
                row = yy * 32 + part * 16
                for side in range(2):
                    piece = back_ref[h, part * 2 + side, pl.ds(yy, 16, stride=16), :]
                    first, second = halves(piece)
                    pair_ref[row : row + 16, side * 128 : side * 128 + 128] = first
                    pair_ref[row : row + 16, N + side * 128 : N + side * 128 + 128] = second

        def step(n, carry):
            k = base + n
            _, l = member(k)
            infos = (g_ref[h, l * 2 + 1 - c, 64:66], g_ref[h, l * 2 + c, 64:66])
            picked = pick_pair(infos, pair_ref[...], table, start)
            for i in range(4):
                mate_out[k, i * 8 : i * 8 + 8] = picked[:, i * 2 * N : i * 2 * N + N]
            pass_on(k).start()
            for i in range(4):
                own_sum[k, i * 8 : i * 8 + 8] = picked[:, i * 2 * N + N : (i + 1) * 2 * N]

            @pl.when(k > 0)
            def _():
                pass_on(k - 1).wait_recv()
                own_sum[k - 1] = own_sum[k - 1] + mate_in[k - 1]
                ring_on(k - 1).start()

            return carry

        lax.fori_loop(0, 4, step, 0)

    pick_half(first_copies, first_own, 1 - zh, 0)
    pick_half(second_copies, second_own, zh, 4)
    pass_on(7).wait_recv()
    total = own_sum[7] + mate_in[7]
    for k in range(7):
        ring_on(k).wait_recv()
        total = total + ring_in[k]
    results(counts_ref, total, weights_ref, out_ref, flip_ref)
    for copy in direct + relays + sent:
        copy.wait_send()
    for k in range(8):
        hand(0, 0, k).wait_send()
        pass_on(k).wait_send()
    for k in range(7):
        ring_on(k).wait_send()


def transform_tables():
    row = np.arange(512)
    h, xy, yy = row // 256, row // 16 % 16, row % 16
    used = (yy < 11).astype(np.float64)
    y = ((h * 16 + xy) * 8 - 1 + yy) % N
    k = np.arange(N)
    angle = 2 * np.pi * (k[:, None] * y[None, :] % N) / N
    cosine, sine = np.cos(angle) * used, np.sin(angle) * used
    forward = np.stack([cosine.reshape(4, 64, 2, N), sine.reshape(4, 64, 2, N)], axis=1)
    forward = forward.transpose(3, 0, 1, 2, 4).reshape(2, 4, 128, N)
    backward = np.stack([cosine.T.reshape(2, 4, 64, N), sine.T.reshape(2, 4, 64, N)], axis=2)
    backward = backward.reshape(2, 4, 128, N)
    angle = 2 * np.pi * (k[:, None] * k[None, :] % N) / N
    high, low = np_halves(np.concatenate([np.cos(angle), np.sin(angle)], axis=1))
    along = np.concatenate([high, low, high], axis=0)
    return np.stack(np_halves(forward)), along, np.stack(np_halves(backward))


def on_device(values, weights, anchors, counts, spectrum):
    dma = pltpu.SemaphoreType.DMA
    anywhere = pl.BlockSpec(memory_space=pl.ANY)
    tables = transform_tables()
    field = pltpu.VMEM((2, 4, 256, 128), F32)
    strided = pltpu.VMEM((2, 4, 272, 128), F32)
    share = pltpu.VMEM((8, 32, N), F32)
    return pl.pallas_call(
        whole_kernel,
        out_shape=jax.ShapeDtypeStruct(values.shape, F32),
        in_specs=[SM, VM, VM] + [anywhere] * 5,
        out_specs=VM,
        scratch_shapes=[
            pltpu.VMEM(weights.shape, F32),
            pltpu.VMEM(spectrum.shape, F32),
            *[pltpu.VMEM(t.shape, BF16) for t in tables],
            pltpu.VMEM((128, 64), F32),
            pltpu.VMEM((2, 8, 72, 128), F32),
            pltpu.VMEM((352, N), F32),
            strided,
            field,
            pltpu.VMEM((4, 128, 2 * N), F32),
            field,
            strided,
            pltpu.VMEM((352, 2 * N), BF16),
            share,
            share,
            share,
            share,
            dma((10,)),
            *[dma((8,))] * 4,
            *[dma((2, 16))] * 4,
            *[dma((8,))] * 4,
        ],
        compiler_params=pltpu.CompilerParams(
            collective_id=1, has_side_effects=True, vmem_limit_bytes=LIMIT
        ),
    )(counts, values, anchors, weights, spectrum, *tables)


def solution(mesh):
    placed = (
        P(None, ("slab", "pencil")),
        P(("slab", "pencil"), None),
        P(None, ("slab", "pencil")),
        P(("slab", "pencil")),
        P(("slab", "pencil"), None, None),
    )
    return jax.shard_map(
        on_device,
        mesh=mesh,
        in_specs=placed,
        out_specs=P(None, ("slab", "pencil")),
        check_vma=False,
    )
```

```python
import math

import jax
import jax.numpy as jnp
import numpy as np
from jax import lax
from jax.experimental import pallas as pl
from jax.experimental.pallas import tpu as pltpu
from jax.sharding import PartitionSpec as P

MESH = pl.DeviceIdType.MESH
VM = pl.BlockSpec(memory_space=pltpu.VMEM)
SM = pl.BlockSpec(memory_space=pltpu.SMEM)
F32 = jnp.float32
BF16 = jnp.bfloat16
N = 256
LIMIT = 56 * 1024 * 1024


def halves(x):
    high = x.astype(BF16)
    low = (x - high.astype(F32)).astype(BF16)
    return high, low


def mm(a, b):
    return jnp.dot(a, b, preferred_element_type=F32)


def mm_nt(a, b):
    return lax.dot_general(a, b, (((1,), (1,)), ((), ())), preferred_element_type=F32)


def left3(high, low):
    return jnp.concatenate([high, high, low], axis=1)


def right3(high, low):
    return jnp.concatenate([high, low, high], axis=0)


def np_halves(x):
    x = np.asarray(x, np.float32)
    high = x.astype(jnp.bfloat16)
    low = (x - high.astype(np.float32)).astype(jnp.bfloat16)
    return high, low


def circle(m):
    x = (jnp.bitwise_and(m, N - 1) - N // 2).astype(F32) * (math.pi / N)
    y = x * x
    sine = jnp.full_like(x, -1.0 / 39916800)
    for f in (362880, -5040, 120, -6, 1):
        sine = sine * y + 1.0 / f
    sine = sine * x
    cosine = jnp.full_like(x, 1.0 / 479001600)
    for f in (-3628800, 40320, -720, 24, -2, 1):
        cosine = cosine * y + 1.0 / f
    return 2.0 * sine * sine - 1.0, -2.0 * sine * cosine


def remote(src, dst, send, recv, device):
    return pltpu.make_async_remote_copy(
        src_ref=src, dst_ref=dst, send_sem=send, recv_sem=recv, device_id=device, device_id_type=MESH
    )


def offset_table(shape, start, spread):
    at0 = lax.broadcasted_iota(jnp.int32, shape, 0)
    at1 = lax.broadcasted_iota(jnp.int32, shape, 1)
    if spread:
        group, span = at0, at1
        piece, span = span // 8, lax.rem(span, 8)
    else:
        group, span = lax.rem(at1, 32), at0
        piece = at1 // 32
    part, freq = group // 16, lax.rem(group, 16) + start
    r, offset = span // 4, lax.rem(span, 4) - 1
    cosine, sine = circle(freq * offset)
    exact = jnp.where(part == r, cosine, jnp.where(part == 0, sine, -sine))
    high = exact.astype(BF16).astype(F32)
    return jnp.where(piece < 2, high, exact - high).astype(BF16)


def phases(x_row, start):
    freq = lax.broadcasted_iota(jnp.int32, (16, x_row.shape[1]), 0) + start
    return circle(freq * x_row.astype(jnp.int32))


def z_hot(z_row):
    grid_z = lax.broadcasted_iota(jnp.int32, (N, z_row.shape[1]), 0)
    return (grid_z == z_row).astype(F32).astype(BF16)


def places(info):
    lane = lax.broadcasted_iota(jnp.int32, (8, 128), 1)
    first = lane < 64
    yz = jnp.broadcast_to(info[0:1], (8, 128))
    x = jnp.broadcast_to(info[1:2], (8, 128))
    zy = pltpu.roll(yz, 64, 1)
    y = jnp.where(first, yz, zy)
    z = jnp.where(first, zy, yz)
    x = jnp.where(first, x, pltpu.roll(x, 64, 1))
    y_row, z_row, x_row = (jnp.concatenate([v, v], axis=1)[0:1] for v in (y, z, x))
    j = lax.broadcasted_iota(jnp.int32, (1, N), 1) // 64
    z_row = jnp.bitwise_and(z_row.astype(jnp.int32) + (j - 1), N - 1)
    return y_row, z_row, x_row


def contributions(counts_ref, values_ref, weights_ref, waits, out_ref, flip_ref):
    for r in range(2):
        for b in range(64):
            flip_ref[r * 64 + b : r * 64 + b + 1, :] = values_ref[r : r + 1, b * 64 : b * 64 + 64]
    lane = lax.broadcasted_iota(jnp.int32, (64, 128), 1)
    first = lane < 64
    v = (flip_ref[:64, :], flip_ref[64:, :])
    totals = [jnp.zeros((64, 128), F32)] * 2
    for t in range(32):
        if t % 8 == 0:
            waits[t // 8].wait()
        tile = weights_ref[:, t * 128 : (t + 1) * 128]
        for r in range(2):
            spread = jnp.where(first, v[r][:, 2 * t : 2 * t + 1], v[r][:, 2 * t + 1 : 2 * t + 2])
            totals[r] = totals[r] + tile * spread
    totals = [t + pltpu.roll(t, 64, 1) for t in totals]
    both = jnp.where(first, totals[0], totals[1])
    row = lax.broadcasted_iota(jnp.int32, (64, 128), 0)
    both = jnp.where(row < counts_ref[0], both, 0.0)
    flipped = both.T
    for i in range(4):
        for j in range(4):
            for r in range(2):
                base = r * 64 + i * 16 + j * 4
                row = j // 2 * 32 + i * 8 + r * 4
                out_ref[row : row + 4, j % 2 * 64 : j % 2 * 64 + 64] = flipped[base : base + 4, :]


def results(counts_ref, picked, weights_ref, out_ref, flip_ref):
    for i in range(4):
        for j in range(4):
            for r in range(2):
                base = r * 64 + i * 16 + j * 4
                flip_ref[base : base + 4, :] = picked[i * 8 + r * 4 : i * 8 + r * 4 + 4, j * 64 : j * 64 + 64]
    both = flip_ref[...].T
    lane = lax.broadcasted_iota(jnp.int32, (64, 128), 1)
    first = lane < 64
    row = lax.broadcasted_iota(jnp.int32, (64, 128), 0)
    both = jnp.where(row < counts_ref[0], both, 0.0)
    turned = pltpu.roll(both, 64, 1)
    picks = (jnp.where(first, both, turned), jnp.where(first, turned, both))
    total = jnp.zeros((128, 64), F32)
    source = lax.broadcasted_iota(jnp.int32, (256, 64), 0) // 64
    target = lax.broadcasted_iota(jnp.int32, (256, 64), 1)
    for t in range(16):
        left = weights_ref[:, t * 256 : t * 256 + 128]
        right = weights_ref[:, t * 256 + 128 : t * 256 + 256]
        product = jnp.concatenate(
            [jnp.concatenate([left * pk, right * pk], axis=1) for pk in picks], axis=0
        )
        high, low = halves(product)
        collect = (target == source + 4 * t).astype(F32).astype(BF16)
        total = total + mm(high, collect) + mm(low, collect)
    for r in range(2):
        for b in range(64):
            out_ref[r : r + 1, b * 64 : b * 64 + 64] = total[r * 64 + b : r * 64 + b + 1, :]


def spread_pair(blocks, table, start, acc_ref):
    rows = [places(b[64:66]) for b in blocks]
    y_row, z_row, x_row = (jnp.concatenate([r[k] for r in rows], axis=1) for k in range(3))
    cosine, sine = phases(x_row, start)
    raw = jnp.concatenate(
        [
            b[k * 32 + i * 8 : k * 32 + i * 8 + 8]
            for i in range(4)
            for b in blocks
            for k in range(2)
        ],
        axis=1,
    )
    high = raw.astype(BF16).astype(F32)
    low = raw - high
    stacked = jnp.concatenate([high, low, high, low], axis=0).astype(BF16)
    flat = mm(table, stacked)
    parts = []
    for i in range(4):
        real = flat[:16, i * 2 * N : (i + 1) * 2 * N]
        imag = flat[16:, i * 2 * N : (i + 1) * 2 * N]
        parts.append(
            jnp.concatenate([cosine * real + sine * imag, cosine * imag - sine * real], axis=0)
        )
    y_all = jnp.broadcast_to(y_row, (32, 2 * N))
    pieces = []
    for yy in range(11):
        piece = jnp.zeros((32, 2 * N), F32)
        for i in range(4):
            if 0 <= yy - i < 8:
                piece = jnp.where(y_all == float(yy - i), parts[i], piece)
        pieces.append(jnp.concatenate(halves(piece), axis=1))
    hot = z_hot(z_row)
    acc_ref[...] += mm_nt(jnp.concatenate(pieces, axis=0), jnp.concatenate([hot, hot], axis=1))


def pick_pair(infos, smooth, table, start):
    rows = [places(info) for info in infos]
    y_row, z_row, x_row = (jnp.concatenate([r[k] for r in rows], axis=1) for k in range(3))
    cosine, sine = phases(x_row, start)
    hot = z_hot(z_row)
    rows = mm(smooth, jnp.concatenate([hot, hot], axis=0))
    y_all = jnp.broadcast_to(y_row, (32, 2 * N))
    turned = []
    for i in range(4):
        piece = rows[i * 32 : (i + 1) * 32]
        for y in range(1, 8):
            piece = jnp.where(y_all == float(y), rows[(y + i) * 32 : (y + i + 1) * 32], piece)
        real, imag = piece[:16], piece[16:]
        turned.append(
            jnp.concatenate([cosine * real - sine * imag, cosine * imag + sine * real], axis=0)
        )
    h, l = halves(jnp.concatenate(turned, axis=1))
    return mm(table, jnp.concatenate([h, l, h, l], axis=0))


def whole_kernel(
    counts_ref,
    values_ref,
    anchors_ref,
    weights_any,
    spectrum_any,
    yt_any,
    zt_any,
    yb_any,
    out_ref,
    weights_ref,
    spectrum_ref,
    yt_ref,
    zt_ref,
    yb_ref,
    flip_ref,
    g_ref,
    acc_ref,
    field_ref,
    landed_ref,
    along_ref,
    piece_ref,
    smooth_ref,
    back_ref,
    pair_ref,
    mate_out,
    mate_in,
    own_sum,
    ring_in,
    local_sem,
    ring_send,
    ring_recv,
    mate_send,
    mate_recv,
    to_send,
    to_recv,
    fro_send,
    fro_recv,
    ring2_send,
    ring2_recv,
    mate2_send,
    mate2_recv,
):
    s = lax.axis_index("slab")
    p = lax.axis_index("pencil")
    zl, c = s // 2, lax.rem(s, 2)
    zh, xy = p // 16, lax.rem(p, 16)
    gx, gy = xy // 4, lax.rem(xy, 4)
    start = s * 32 + zh * 16
    mate = (zl * 2 + 1 - c, p)

    def chip(q, t):
        to = lax.rem(gx + q, 4) * 4 + lax.rem(gy + t, 4)
        return to, (s, zh * 16 + to)

    def ring_device(h, l):
        return l * 2 + c, h * 16 + xy

    loads = []
    for k in range(4):
        cols = pl.ds(k * 1024, 1024)
        loads.append(
            pltpu.make_async_copy(weights_any.at[:, cols], weights_ref.at[:, cols], local_sem.at[k])
        )
    tables = [
        pltpu.make_async_copy(src, dst, local_sem.at[4 + k])
        for k, (src, dst) in enumerate(
            [
                (spectrum_any, spectrum_ref),
                (yt_any, yt_ref),
                (zt_any, zt_ref),
                (yb_any, yb_ref),
            ]
        )
    ]
    for load in loads + tables:
        load.start()
    landed_ref[...] = jnp.zeros_like(landed_ref)

    sending = [(2, 2), (1, 2), (2, 1), (3, 2), (2, 3), (1, 1), (3, 3), (1, 3), (3, 1), (2, 0)]
    sending += [(0, 2), (1, 0), (0, 1), (3, 0), (0, 3)]
    barrier = pltpu.get_barrier_semaphore()

    def greet(device):
        pl.semaphore_signal(barrier, inc=1, device_id=device, device_id_type=MESH)

    for k in (0, 1, 3, 2):
        greet(ring_device(1 - zh, lax.rem(zl + k, 4)))
    for q, t in sending:
        greet(chip(q, t)[1])
    for k in (1, 3, 2):
        greet(ring_device(zh, lax.rem(zl + k, 4)))
    greet(mate)
    acc_ref[...] = jnp.zeros_like(acc_ref)

    mine = g_ref.at[zh, s]
    contributions(counts_ref, values_ref, weights_ref, loads, mine, flip_ref)
    mine[64:65, :64] = (anchors_ref[0:1, :] - p * 8).astype(F32)
    mine[64:65, 64:] = anchors_ref[1:2, :].astype(F32)
    mine[65:66, :64] = anchors_ref[2:3, :].astype(F32)
    mine[65:66, 64:] = anchors_ref[2:3, :].astype(F32)
    pl.semaphore_wait(barrier, 23)

    def block(h, d):
        return g_ref.at[h, d, pl.ds(0, 66)]

    def hand(h, d, k):
        return remote(block(h, d), block(h, d), mate_send.at[k], mate_recv.at[k], mate)

    def source(k):
        same = k < 4
        h = jnp.where(same, zh, 1 - zh)
        return h, lax.rem(zl + 8 - k, 4) * 2 + c

    z = zh * 4 + zl

    def along_ring(t):
        to = lax.rem(z + 8 + t, 8)
        return ring_device(to // 4, lax.rem(to, 4))

    def place_of(t):
        at = lax.rem(z + 8 + t, 8)
        return block(at // 4, lax.rem(at, 4) * 2 + c)

    def step_on(t, u, k):
        slot = lax.rem(u - t + 8, 8)
        return remote(
            place_of(t), place_of(t), ring_send.at[k], ring_recv.at[slot], along_ring(u)
        )

    def landed_from(t):
        slot = lax.rem(8 - t, 8)
        return remote(place_of(t), place_of(t), ring_send.at[0], ring_recv.at[slot], mate)

    way = 1 - 2 * lax.rem(z, 2)
    direct = [step_on(0, u, k) for k, u in enumerate((2, -2, 1, -1))]
    relays = [step_on(-2, 1, 4), step_on(2, -1, 5), step_on(-2 * way, 2 * way, 6)]

    def arrive(k):
        h, d = source(k)
        back = lax.rem(z - h * 4 - d // 2 + 8, 8)

        @pl.when(jnp.logical_and(back != 2, back != 6))
        def _():
            place = block(h, d)
            remote(place, place, ring_send.at[0], ring_recv.at[back], mate).wait_recv()

        hand(h, d, k).start()

    for copy in direct:
        copy.start()
    hand(zh, s, 0).start()
    table = offset_table((32, 32), start, True)

    def turn_of(n):
        return jnp.where(n < 4, n, 4 + lax.rem(n + 1, 4))

    def gather_step(n, carry):
        @pl.when(jnp.logical_and(n > 0, n < 7))
        def _():
            arrive(turn_of(n + 1))

        k = turn_of(n)
        h, d = source(k)
        mate_d = d + 1 - 2 * c
        hand(h, mate_d, k).wait_recv()
        spread_pair((g_ref.at[h, d], g_ref.at[h, mate_d]), table, start, acc_ref)

        @pl.when(n == 0)
        def _():
            landed_from(-2).wait_recv()
            landed_from(2).wait_recv()
            for copy in relays:
                copy.start()
            arrive(1)

        return carry

    def rows_of(ref, h, to):
        return ref.at[h, :, pl.ds(to * 16, 11)]

    def send_half(turn, h):
        for yy in range(11):
            for part in range(2):
                base = yy * 32 + part * 16
                for side in range(2):
                    field_ref[h, part * 2 + side, pl.ds(yy, 16, stride=16), :] = acc_ref[
                        base : base + 16, side * 128 : side * 128 + 128
                    ]
        copies = []
        for q, t in sending:
            to, device = chip(q, t)
            k = q * 4 + t
            copy = remote(
                rows_of(field_ref, h, to),
                rows_of(landed_ref, h, xy),
                to_send.at[turn, k],
                to_recv.at[turn, k],
                device,
            )
            copy.start()
            copies.append(copy)
        own = pltpu.make_async_copy(
            rows_of(field_ref, h, xy), rows_of(landed_ref, h, xy), local_sem.at[8 + turn]
        )
        own.start()
        return copies, own

    lax.fori_loop(0, 4, gather_step, 0)
    first_copies, first_own = send_half(0, zh)
    acc_ref[...] = jnp.zeros_like(acc_ref)
    lax.fori_loop(4, 8, gather_step, 0)
    second_copies, second_own = send_half(1, 1 - zh)
    for load in tables:
        load.wait()

    def landed(h, copies, own):
        own.wait()
        for q in (1, 3, 2, 0):
            for (to_q, _), copy in zip(sending, copies):
                if to_q == q:
                    copy.wait_recv()
            row = pl.multiple_of(lax.rem(gx + 4 - q, 4) * 64, 64)
            for k in range(4):
                high, low = halves(landed_ref[h, k, pl.ds(row, 64)])
                lanes = slice(k * 128, k * 128 + 128)
                piece_ref[0, pl.ds(row, 64), lanes] = high
                piece_ref[1, pl.ds(row, 64), lanes] = low
                piece_ref[2, pl.ds(row, 64), lanes] = high
        return piece_ref[...].reshape(3 * N, 2 * N)

    fields = landed(zh, first_copies, first_own)
    for n in range(4):
        along_ref[n] = mm(left3(yt_ref[0, zh, n], yt_ref[1, zh, n]), fields)
    fields = landed(1 - zh, second_copies, second_own)
    z_table = zt_ref[...]
    highs, lows = [], []
    for n in range(4):
        u = along_ref[n] + mm(left3(yt_ref[0, 1 - zh, n], yt_ref[1, 1 - zh, n]), fields)
        real = u[:64, :N] + u[64:, N:]
        imag = u[:64, N:] - u[64:, :N]
        u = mm(left3(*halves(jnp.concatenate([real, imag], axis=0))), z_table)
        scale = spectrum_ref[0, n * 64 : n * 64 + 64] * (1.0 / (N * N * N))
        real = (u[:64, :N] + u[64:, N:]) * scale
        imag = (u[64:, :N] - u[:64, N:]) * scale
        u = mm(left3(*halves(jnp.concatenate([real, imag], axis=0))), z_table)
        real = u[:64, :N] - u[64:, N:]
        imag = u[64:, :N] + u[:64, N:]
        h, l = halves(jnp.concatenate([real, imag], axis=1))
        highs.append(h)
        lows.append(l)
    fields = right3(jnp.concatenate(highs, axis=0), jnp.concatenate(lows, axis=0))

    def return_half(turn, h):
        copies = []
        for q in (2, 1, 3, 0):
            column = lax.rem(gx + q, 4)
            u = mm(left3(yb_ref[0, h, column], yb_ref[1, h, column]), fields)
            real = u[:64, :N] - u[64:, N:]
            imag = u[:64, N:] + u[64:, :N]
            rows = pl.ds(column * 64, 64)
            smooth_ref[h, 0, rows] = real[:, :128]
            smooth_ref[h, 1, rows] = real[:, 128:]
            smooth_ref[h, 2, rows] = imag[:, :128]
            smooth_ref[h, 3, rows] = imag[:, 128:]
            for t in (1, 3, 2, 0):
                if (q, t) == (0, 0):
                    continue
                to, device = chip(q, t)
                k = q * 4 + t
                copy = remote(
                    rows_of(smooth_ref, h, to),
                    rows_of(back_ref, h, xy),
                    fro_send.at[turn, k],
                    fro_recv.at[turn, k],
                    device,
                )
                copy.start()
                copies.append(copy)
        own = pltpu.make_async_copy(
            rows_of(smooth_ref, h, xy), rows_of(back_ref, h, xy), local_sem.at[8 + turn]
        )
        own.start()
        return copies, own

    sent = first_copies + second_copies
    first_copies, first_own = return_half(0, 1 - zh)
    second_copies, second_own = return_half(1, zh)
    sent = sent + first_copies + second_copies
    table = offset_table((8, 128), start, False)

    def member(k):
        other = k < 4
        h = jnp.where(other, 1 - zh, zh)
        return h, jnp.where(other, lax.rem(zl + k, 4), lax.rem(zl + k + 1, 4))

    def pass_on(k):
        return remote(mate_out.at[k], mate_in.at[k], mate2_send.at[k], mate2_recv.at[k], mate)

    def ring_on(k):
        h, l = member(k)
        return remote(
            own_sum.at[k], ring_in.at[k], ring2_send.at[k], ring2_recv.at[k], ring_device(h, l)
        )

    def pick_half(copies, own, h, base):
        own.wait()
        for copy in copies:
            copy.wait_recv()
        for yy in range(11):
            for part in range(2):
                row = yy * 32 + part * 16
                for side in range(2):
                    piece = back_ref[h, part * 2 + side, pl.ds(yy, 16, stride=16), :]
                    first, second = halves(piece)
                    pair_ref[row : row + 16, side * 128 : side * 128 + 128] = first
                    pair_ref[row : row + 16, N + side * 128 : N + side * 128 + 128] = second

        def step(n, carry):
            k = base + n
            _, l = member(k)
            infos = (g_ref[h, l * 2 + 1 - c, 64:66], g_ref[h, l * 2 + c, 64:66])
            picked = pick_pair(infos, pair_ref[...], table, start)
            for i in range(4):
                mate_out[k, i * 8 : i * 8 + 8] = picked[:, i * 2 * N : i * 2 * N + N]
            pass_on(k).start()
            for i in range(4):
                own_sum[k, i * 8 : i * 8 + 8] = picked[:, i * 2 * N + N : (i + 1) * 2 * N]

            @pl.when(k > 0)
            def _():
                pass_on(k - 1).wait_recv()
                own_sum[k - 1] = own_sum[k - 1] + mate_in[k - 1]
                ring_on(k - 1).start()

            return carry

        lax.fori_loop(0, 4, step, 0)

    pick_half(first_copies, first_own, 1 - zh, 0)
    pick_half(second_copies, second_own, zh, 4)
    pass_on(7).wait_recv()
    total = own_sum[7] + mate_in[7]
    for k in range(7):
        ring_on(k).wait_recv()
        total = total + ring_in[k]
    results(counts_ref, total, weights_ref, out_ref, flip_ref)
    for copy in direct + relays + sent:
        copy.wait_send()
    for k in range(8):
        hand(0, 0, k).wait_send()
        pass_on(k).wait_send()
    for k in range(7):
        ring_on(k).wait_send()


def transform_tables():
    row = np.arange(512)
    h, xy, yy = row // 256, row // 16 % 16, row % 16
    used = (yy < 11).astype(np.float64)
    y = ((h * 16 + xy) * 8 - 1 + yy) % N
    k = np.arange(N)
    angle = 2 * np.pi * (k[:, None] * y[None, :] % N) / N
    cosine, sine = np.cos(angle) * used, np.sin(angle) * used
    forward = np.stack([cosine.reshape(4, 64, 2, N), sine.reshape(4, 64, 2, N)], axis=1)
    forward = forward.transpose(3, 0, 1, 2, 4).reshape(2, 4, 128, N)
    backward = np.stack([cosine.T.reshape(2, 4, 64, N), sine.T.reshape(2, 4, 64, N)], axis=2)
    backward = backward.reshape(2, 4, 128, N)
    angle = 2 * np.pi * (k[:, None] * k[None, :] % N) / N
    high, low = np_halves(np.concatenate([np.cos(angle), np.sin(angle)], axis=1))
    along = np.concatenate([high, low, high], axis=0)
    return np.stack(np_halves(forward)), along, np.stack(np_halves(backward))


def on_device(values, weights, anchors, counts, spectrum):
    dma = pltpu.SemaphoreType.DMA
    anywhere = pl.BlockSpec(memory_space=pl.ANY)
    tables = transform_tables()
    field = pltpu.VMEM((2, 4, 256, 128), F32)
    strided = pltpu.VMEM((2, 4, 272, 128), F32)
    share = pltpu.VMEM((8, 32, N), F32)
    return pl.pallas_call(
        whole_kernel,
        out_shape=jax.ShapeDtypeStruct(values.shape, F32),
        in_specs=[SM, VM, VM] + [anywhere] * 5,
        out_specs=VM,
        scratch_shapes=[
            pltpu.VMEM(weights.shape, F32),
            pltpu.VMEM(spectrum.shape, F32),
            *[pltpu.VMEM(t.shape, BF16) for t in tables],
            pltpu.VMEM((128, 64), F32),
            pltpu.VMEM((2, 8, 72, 128), F32),
            pltpu.VMEM((352, N), F32),
            strided,
            field,
            pltpu.VMEM((4, 128, 2 * N), F32),
            pltpu.VMEM((3, N, 2 * N), BF16),
            field,
            strided,
            pltpu.VMEM((352, 2 * N), BF16),
            share,
            share,
            share,
            share,
            dma((10,)),
            *[dma((8,))] * 4,
            *[dma((2, 16))] * 4,
            *[dma((8,))] * 4,
        ],
        compiler_params=pltpu.CompilerParams(
            collective_id=1, has_side_effects=True, vmem_limit_bytes=LIMIT
        ),
    )(counts, values, anchors, weights, spectrum, *tables)


def solution(mesh):
    placed = (
        P(None, ("slab", "pencil")),
        P(("slab", "pencil"), None),
        P(None, ("slab", "pencil")),
        P(("slab", "pencil")),
        P(("slab", "pencil"), None, None),
    )
    return jax.shard_map(
        on_device,
        mesh=mesh,
        in_specs=placed,
        out_specs=P(None, ("slab", "pencil")),
        check_vma=False,
    )
```

```python
import math

import jax
import jax.numpy as jnp
import numpy as np
from jax import lax
from jax.experimental import pallas as pl
from jax.experimental.pallas import tpu as pltpu
from jax.sharding import PartitionSpec as P

MESH = pl.DeviceIdType.MESH
VM = pl.BlockSpec(memory_space=pltpu.VMEM)
SM = pl.BlockSpec(memory_space=pltpu.SMEM)
F32 = jnp.float32
BF16 = jnp.bfloat16
N = 256
LIMIT = 56 * 1024 * 1024


def halves(x):
    high = x.astype(BF16)
    low = (x - high.astype(F32)).astype(BF16)
    return high, low


def mm(a, b):
    return jnp.dot(a, b, preferred_element_type=F32)


def mm_nt(a, b):
    return lax.dot_general(a, b, (((1,), (1,)), ((), ())), preferred_element_type=F32)


def left3(high, low):
    return jnp.concatenate([high, high, low], axis=1)


def right3(high, low):
    return jnp.concatenate([high, low, high], axis=0)


def np_halves(x):
    x = np.asarray(x, np.float32)
    high = x.astype(jnp.bfloat16)
    low = (x - high.astype(np.float32)).astype(jnp.bfloat16)
    return high, low


def circle(m):
    x = (jnp.bitwise_and(m, N - 1) - N // 2).astype(F32) * (math.pi / N)
    y = x * x
    sine = jnp.full_like(x, -1.0 / 39916800)
    for f in (362880, -5040, 120, -6, 1):
        sine = sine * y + 1.0 / f
    sine = sine * x
    cosine = jnp.full_like(x, 1.0 / 479001600)
    for f in (-3628800, 40320, -720, 24, -2, 1):
        cosine = cosine * y + 1.0 / f
    return 2.0 * sine * sine - 1.0, -2.0 * sine * cosine


def remote(src, dst, send, recv, device):
    return pltpu.make_async_remote_copy(
        src_ref=src, dst_ref=dst, send_sem=send, recv_sem=recv, device_id=device, device_id_type=MESH
    )


def offset_table(shape, start, spread):
    at0 = lax.broadcasted_iota(jnp.int32, shape, 0)
    at1 = lax.broadcasted_iota(jnp.int32, shape, 1)
    if spread:
        group, span = at0, at1
        piece, span = span // 8, lax.rem(span, 8)
    else:
        group, span = lax.rem(at1, 32), at0
        piece = at1 // 32
    part, freq = group // 16, lax.rem(group, 16) + start
    r, offset = span // 4, lax.rem(span, 4) - 1
    cosine, sine = circle(freq * offset)
    exact = jnp.where(part == r, cosine, jnp.where(part == 0, sine, -sine))
    high = exact.astype(BF16).astype(F32)
    return jnp.where(piece < 2, high, exact - high).astype(BF16)


def phases(x_row, start):
    freq = lax.broadcasted_iota(jnp.int32, (16, x_row.shape[1]), 0) + start
    return circle(freq * x_row.astype(jnp.int32))


def z_hot(z_row):
    grid_z = lax.broadcasted_iota(jnp.int32, (N, z_row.shape[1]), 0)
    return (grid_z == z_row).astype(F32).astype(BF16)


def places(info):
    lane = lax.broadcasted_iota(jnp.int32, (8, 128), 1)
    first = lane < 64
    yz = jnp.broadcast_to(info[0:1], (8, 128))
    x = jnp.broadcast_to(info[1:2], (8, 128))
    zy = pltpu.roll(yz, 64, 1)
    y = jnp.where(first, yz, zy)
    z = jnp.where(first, zy, yz)
    x = jnp.where(first, x, pltpu.roll(x, 64, 1))
    y_row, z_row, x_row = (jnp.concatenate([v, v], axis=1)[0:1] for v in (y, z, x))
    j = lax.broadcasted_iota(jnp.int32, (1, N), 1) // 64
    z_row = jnp.bitwise_and(z_row.astype(jnp.int32) + (j - 1), N - 1)
    return y_row, z_row, x_row


def contributions(counts_ref, values_ref, weights_ref, waits, out_ref, flip_ref):
    for r in range(2):
        for b in range(64):
            flip_ref[r * 64 + b : r * 64 + b + 1, :] = values_ref[r : r + 1, b * 64 : b * 64 + 64]
    lane = lax.broadcasted_iota(jnp.int32, (64, 128), 1)
    first = lane < 64
    v = (flip_ref[:64, :], flip_ref[64:, :])
    totals = [jnp.zeros((64, 128), F32)] * 2
    for t in range(32):
        if t % 8 == 0:
            waits[t // 8].wait()
        tile = weights_ref[:, t * 128 : (t + 1) * 128]
        for r in range(2):
            spread = jnp.where(first, v[r][:, 2 * t : 2 * t + 1], v[r][:, 2 * t + 1 : 2 * t + 2])
            totals[r] = totals[r] + tile * spread
    totals = [t + pltpu.roll(t, 64, 1) for t in totals]
    both = jnp.where(first, totals[0], totals[1])
    row = lax.broadcasted_iota(jnp.int32, (64, 128), 0)
    both = jnp.where(row < counts_ref[0], both, 0.0)
    flipped = both.T
    for i in range(4):
        for j in range(4):
            for r in range(2):
                base = r * 64 + i * 16 + j * 4
                row = j // 2 * 32 + i * 8 + r * 4
                out_ref[row : row + 4, j % 2 * 64 : j % 2 * 64 + 64] = flipped[base : base + 4, :]


def results(counts_ref, picked, weights_ref, out_ref, flip_ref):
    for i in range(4):
        for j in range(4):
            for r in range(2):
                base = r * 64 + i * 16 + j * 4
                flip_ref[base : base + 4, :] = picked[i * 8 + r * 4 : i * 8 + r * 4 + 4, j * 64 : j * 64 + 64]
    both = flip_ref[...].T
    lane = lax.broadcasted_iota(jnp.int32, (64, 128), 1)
    first = lane < 64
    row = lax.broadcasted_iota(jnp.int32, (64, 128), 0)
    both = jnp.where(row < counts_ref[0], both, 0.0)
    turned = pltpu.roll(both, 64, 1)
    picks = (jnp.where(first, both, turned), jnp.where(first, turned, both))
    total = jnp.zeros((128, 64), F32)
    source = lax.broadcasted_iota(jnp.int32, (256, 64), 0) // 64
    target = lax.broadcasted_iota(jnp.int32, (256, 64), 1)
    for t in range(16):
        left = weights_ref[:, t * 256 : t * 256 + 128]
        right = weights_ref[:, t * 256 + 128 : t * 256 + 256]
        product = jnp.concatenate(
            [jnp.concatenate([left * pk, right * pk], axis=1) for pk in picks], axis=0
        )
        high, low = halves(product)
        collect = (target == source + 4 * t).astype(F32).astype(BF16)
        total = total + mm(high, collect) + mm(low, collect)
    for r in range(2):
        for b in range(64):
            out_ref[r : r + 1, b * 64 : b * 64 + 64] = total[r * 64 + b : r * 64 + b + 1, :]


def spread_pair(blocks, table, start, acc_ref):
    rows = [places(b[64:66]) for b in blocks]
    y_row, z_row, x_row = (jnp.concatenate([r[k] for r in rows], axis=1) for k in range(3))
    cosine, sine = phases(x_row, start)
    raw = jnp.concatenate(
        [
            b[k * 32 + i * 8 : k * 32 + i * 8 + 8]
            for i in range(4)
            for b in blocks
            for k in range(2)
        ],
        axis=1,
    )
    high = raw.astype(BF16).astype(F32)
    low = raw - high
    stacked = jnp.concatenate([high, low, high, low], axis=0).astype(BF16)
    flat = mm(table, stacked)
    parts = []
    for i in range(4):
        real = flat[:16, i * 2 * N : (i + 1) * 2 * N]
        imag = flat[16:, i * 2 * N : (i + 1) * 2 * N]
        parts.append(
            jnp.concatenate([cosine * real + sine * imag, cosine * imag - sine * real], axis=0)
        )
    y_all = jnp.broadcast_to(y_row, (32, 2 * N))
    pieces = []
    for yy in range(11):
        piece = jnp.zeros((32, 2 * N), F32)
        for i in range(4):
            if 0 <= yy - i < 8:
                piece = jnp.where(y_all == float(yy - i), parts[i], piece)
        pieces.append(jnp.concatenate(halves(piece), axis=1))
    hot = z_hot(z_row)
    acc_ref[...] += mm_nt(jnp.concatenate(pieces, axis=0), jnp.concatenate([hot, hot], axis=1))


def pick_pair(infos, smooth, table, start):
    rows = [places(info) for info in infos]
    y_row, z_row, x_row = (jnp.concatenate([r[k] for r in rows], axis=1) for k in range(3))
    cosine, sine = phases(x_row, start)
    hot = z_hot(z_row)
    rows = mm(smooth, jnp.concatenate([hot, hot], axis=0))
    y_all = jnp.broadcast_to(y_row, (32, 2 * N))
    turned = []
    for i in range(4):
        piece = rows[i * 32 : (i + 1) * 32]
        for y in range(1, 8):
            piece = jnp.where(y_all == float(y), rows[(y + i) * 32 : (y + i + 1) * 32], piece)
        real, imag = piece[:16], piece[16:]
        turned.append(
            jnp.concatenate([cosine * real - sine * imag, cosine * imag + sine * real], axis=0)
        )
    h, l = halves(jnp.concatenate(turned, axis=1))
    return mm(table, jnp.concatenate([h, l, h, l], axis=0))


def whole_kernel(
    counts_ref,
    values_ref,
    anchors_ref,
    weights_any,
    spectrum_any,
    yt_any,
    zt_any,
    yb_any,
    out_ref,
    weights_ref,
    spectrum_ref,
    yt_ref,
    zt_ref,
    yb_ref,
    flip_ref,
    g_ref,
    acc_ref,
    field_ref,
    landed_ref,
    along_ref,
    smooth_ref,
    back_ref,
    pair_ref,
    mate_out,
    mate_in,
    own_sum,
    ring_in,
    local_sem,
    ring_send,
    ring_recv,
    mate_send,
    mate_recv,
    to_send,
    to_recv,
    fro_send,
    fro_recv,
    ring2_send,
    ring2_recv,
    mate2_send,
    mate2_recv,
):
    s = lax.axis_index("slab")
    p = lax.axis_index("pencil")
    zl, c = s // 2, lax.rem(s, 2)
    zh, xy = p // 16, lax.rem(p, 16)
    gx, gy = xy // 4, lax.rem(xy, 4)
    start = s * 32 + zh * 16
    mate = (zl * 2 + 1 - c, p)

    def chip(q, t):
        to = lax.rem(gx + q, 4) * 4 + lax.rem(gy + t, 4)
        return to, (s, zh * 16 + to)

    def ring_device(h, l):
        return l * 2 + c, h * 16 + xy

    loads = []
    for k in range(4):
        cols = pl.ds(k * 1024, 1024)
        loads.append(
            pltpu.make_async_copy(weights_any.at[:, cols], weights_ref.at[:, cols], local_sem.at[k])
        )
    tables = [
        pltpu.make_async_copy(src, dst, local_sem.at[4 + k])
        for k, (src, dst) in enumerate(
            [
                (spectrum_any, spectrum_ref),
                (yt_any, yt_ref),
                (zt_any, zt_ref),
                (yb_any, yb_ref),
            ]
        )
    ]
    for load in loads + tables:
        load.start()
    landed_ref[...] = jnp.zeros_like(landed_ref)

    sending = [(2, 2), (1, 2), (2, 1), (3, 2), (2, 3), (1, 1), (3, 3), (1, 3), (3, 1), (2, 0)]
    sending += [(0, 2), (1, 0), (0, 1), (3, 0), (0, 3)]
    barrier = pltpu.get_barrier_semaphore()

    def greet(device):
        pl.semaphore_signal(barrier, inc=1, device_id=device, device_id_type=MESH)

    for k in (0, 1, 3, 2):
        greet(ring_device(1 - zh, lax.rem(zl + k, 4)))
    for q, t in sending:
        greet(chip(q, t)[1])
    for k in (1, 3, 2):
        greet(ring_device(zh, lax.rem(zl + k, 4)))
    greet(mate)
    acc_ref[...] = jnp.zeros_like(acc_ref)

    mine = g_ref.at[zh, s]
    contributions(counts_ref, values_ref, weights_ref, loads, mine, flip_ref)
    mine[64:65, :64] = (anchors_ref[0:1, :] - p * 8).astype(F32)
    mine[64:65, 64:] = anchors_ref[1:2, :].astype(F32)
    mine[65:66, :64] = anchors_ref[2:3, :].astype(F32)
    mine[65:66, 64:] = anchors_ref[2:3, :].astype(F32)
    pl.semaphore_wait(barrier, 23)

    def block(h, d):
        return g_ref.at[h, d, pl.ds(0, 66)]

    def hand(h, d, k):
        return remote(block(h, d), block(h, d), mate_send.at[k], mate_recv.at[k], mate)

    def source(k):
        same = k < 4
        h = jnp.where(same, zh, 1 - zh)
        return h, lax.rem(zl + 8 - k, 4) * 2 + c

    z = zh * 4 + zl

    def along_ring(t):
        to = lax.rem(z + 8 + t, 8)
        return ring_device(to // 4, lax.rem(to, 4))

    def place_of(t):
        at = lax.rem(z + 8 + t, 8)
        return block(at // 4, lax.rem(at, 4) * 2 + c)

    def step_on(t, u, k):
        slot = lax.rem(u - t + 8, 8)
        return remote(
            place_of(t), place_of(t), ring_send.at[k], ring_recv.at[slot], along_ring(u)
        )

    def landed_from(t):
        slot = lax.rem(8 - t, 8)
        return remote(place_of(t), place_of(t), ring_send.at[0], ring_recv.at[slot], mate)

    way = 1 - 2 * lax.rem(z, 2)
    direct = [step_on(0, u, k) for k, u in enumerate((2, -2, 1, -1))]
    relays = [step_on(-2, 1, 4), step_on(2, -1, 5), step_on(-2 * way, 2 * way, 6)]

    def arrive(k):
        h, d = source(k)
        back = lax.rem(z - h * 4 - d // 2 + 8, 8)

        @pl.when(jnp.logical_and(back != 2, back != 6))
        def _():
            place = block(h, d)
            remote(place, place, ring_send.at[0], ring_recv.at[back], mate).wait_recv()

        hand(h, d, k).start()

    for copy in direct:
        copy.start()
    hand(zh, s, 0).start()
    table = offset_table((32, 32), start, True)

    def turn_of(n):
        m = lax.rem(n, 4)
        inner = jnp.where(m >= 2, 5 - m, m)
        own_half = jnp.where(zl == 3, m, jnp.where(zl == 0, lax.rem(4 - m, 4), inner))
        inner = jnp.where(m == 2, 7, jnp.where(m == 3, 4, 6 - m))
        other = jnp.where(zl == 3, 7 - m, jnp.where(zl == 0, 4 + lax.rem(m + 1, 4), inner))
        return jnp.where(n < 4, own_half, other)

    def gather_step(n, carry):
        @pl.when(jnp.logical_and(n != 3, n < 7))
        def _():
            arrive(turn_of(n + 1))

        k = turn_of(n)
        h, d = source(k)
        mate_d = d + 1 - 2 * c
        hand(h, mate_d, k).wait_recv()
        spread_pair((g_ref.at[h, d], g_ref.at[h, mate_d]), table, start, acc_ref)

        @pl.when(n == 0)
        def _():
            landed_from(-2).wait_recv()
            landed_from(2).wait_recv()
            for copy in relays:
                copy.start()

        return carry

    def rows_of(ref, h, to):
        return ref.at[h, :, pl.ds(to * 16, 11)]

    def send_half(turn, h):
        for yy in range(11):
            for part in range(2):
                base = yy * 32 + part * 16
                for side in range(2):
                    field_ref[h, part * 2 + side, pl.ds(yy, 16, stride=16), :] = acc_ref[
                        base : base + 16, side * 128 : side * 128 + 128
                    ]
        copies = []
        for q, t in sending:
            to, device = chip(q, t)
            k = q * 4 + t
            copy = remote(
                rows_of(field_ref, h, to),
                rows_of(landed_ref, h, xy),
                to_send.at[turn, k],
                to_recv.at[turn, k],
                device,
            )
            copy.start()
            copies.append(copy)
        own = pltpu.make_async_copy(
            rows_of(field_ref, h, xy), rows_of(landed_ref, h, xy), local_sem.at[8 + turn]
        )
        own.start()
        return copies, own

    lax.fori_loop(0, 4, gather_step, 0)
    first_copies, first_own = send_half(0, zh)
    acc_ref[...] = jnp.zeros_like(acc_ref)
    arrive(turn_of(4))
    lax.fori_loop(4, 8, gather_step, 0)
    second_copies, second_own = send_half(1, 1 - zh)
    for load in tables:
        load.wait()

    def landed(h):
        return right3(*halves(jnp.concatenate([landed_ref[h, k] for k in range(4)], axis=1)))

    first_own.wait()
    for copy in first_copies:
        copy.wait_recv()
    fields = landed(zh)
    for n in range(2):
        along_ref[n] = mm(left3(yt_ref[0, zh, n], yt_ref[1, zh, n]), fields)
    second_own.wait()
    for copy in second_copies:
        copy.wait_recv()
    fields = landed(1 - zh)
    z_table = zt_ref[...]
    highs, lows = [], []
    for n in range(2):
        u = along_ref[n] + mm(left3(yt_ref[0, 1 - zh, n], yt_ref[1, 1 - zh, n]), fields)
        real = u[:128, :N] + u[128:, N:]
        imag = u[:128, N:] - u[128:, :N]
        u = mm(left3(*halves(jnp.concatenate([real, imag], axis=0))), z_table)
        scale = spectrum_ref[0, n * 128 : n * 128 + 128] * (1.0 / (N * N * N))
        real = (u[:128, :N] + u[128:, N:]) * scale
        imag = (u[128:, :N] - u[:128, N:]) * scale
        u = mm(left3(*halves(jnp.concatenate([real, imag], axis=0))), z_table)
        real = u[:128, :N] - u[128:, N:]
        imag = u[128:, :N] + u[:128, N:]
        h, l = halves(jnp.concatenate([real, imag], axis=1))
        highs.append(h)
        lows.append(l)
    fields = right3(jnp.concatenate(highs, axis=0), jnp.concatenate(lows, axis=0))

    def return_half(turn, h):
        copies = []
        for q in (2, 1, 3, 0):
            column = lax.rem(gx + q, 4)
            u = mm(left3(yb_ref[0, h, column], yb_ref[1, h, column]), fields)
            real = u[:64, :N] - u[64:, N:]
            imag = u[:64, N:] + u[64:, :N]
            rows = pl.ds(column * 64, 64)
            smooth_ref[h, 0, rows] = real[:, :128]
            smooth_ref[h, 1, rows] = real[:, 128:]
            smooth_ref[h, 2, rows] = imag[:, :128]
            smooth_ref[h, 3, rows] = imag[:, 128:]
            for t in (1, 3, 2, 0):
                if (q, t) == (0, 0):
                    continue
                to, device = chip(q, t)
                k = q * 4 + t
                copy = remote(
                    rows_of(smooth_ref, h, to),
                    rows_of(back_ref, h, xy),
                    fro_send.at[turn, k],
                    fro_recv.at[turn, k],
                    device,
                )
                copy.start()
                copies.append(copy)
        own = pltpu.make_async_copy(
            rows_of(smooth_ref, h, xy), rows_of(back_ref, h, xy), local_sem.at[8 + turn]
        )
        own.start()
        return copies, own

    sent = first_copies + second_copies
    first_copies, first_own = return_half(0, 1 - zh)
    second_copies, second_own = return_half(1, zh)
    sent = sent + first_copies + second_copies
    table = offset_table((8, 128), start, False)

    def member(k):
        other = k < 4
        h = jnp.where(other, 1 - zh, zh)
        return h, jnp.where(other, lax.rem(zl + k, 4), lax.rem(zl + k + 1, 4))

    def pass_on(k):
        return remote(mate_out.at[k], mate_in.at[k], mate2_send.at[k], mate2_recv.at[k], mate)

    def ring_on(k):
        h, l = member(k)
        return remote(
            own_sum.at[k], ring_in.at[k], ring2_send.at[k], ring2_recv.at[k], ring_device(h, l)
        )

    def pick_half(copies, own, h, base):
        own.wait()
        for copy in copies:
            copy.wait_recv()
        for yy in range(11):
            for part in range(2):
                row = yy * 32 + part * 16
                for side in range(2):
                    piece = back_ref[h, part * 2 + side, pl.ds(yy, 16, stride=16), :]
                    first, second = halves(piece)
                    pair_ref[row : row + 16, side * 128 : side * 128 + 128] = first
                    pair_ref[row : row + 16, N + side * 128 : N + side * 128 + 128] = second

        def step(n, carry):
            k = base + n
            _, l = member(k)
            infos = (g_ref[h, l * 2 + 1 - c, 64:66], g_ref[h, l * 2 + c, 64:66])
            picked = pick_pair(infos, pair_ref[...], table, start)
            for i in range(4):
                mate_out[k, i * 8 : i * 8 + 8] = picked[:, i * 2 * N : i * 2 * N + N]
            pass_on(k).start()
            for i in range(4):
                own_sum[k, i * 8 : i * 8 + 8] = picked[:, i * 2 * N + N : (i + 1) * 2 * N]

            @pl.when(k > 0)
            def _():
                pass_on(k - 1).wait_recv()
                own_sum[k - 1] = own_sum[k - 1] + mate_in[k - 1]
                ring_on(k - 1).start()

            return carry

        lax.fori_loop(0, 4, step, 0)

    pick_half(first_copies, first_own, 1 - zh, 0)
    pick_half(second_copies, second_own, zh, 4)
    pass_on(7).wait_recv()
    total = own_sum[7] + mate_in[7]
    for k in range(7):
        ring_on(k).wait_recv()
        total = total + ring_in[k]
    results(counts_ref, total, weights_ref, out_ref, flip_ref)
    for copy in direct + relays + sent:
        copy.wait_send()
    for k in range(8):
        hand(0, 0, k).wait_send()
        pass_on(k).wait_send()
    for k in range(7):
        ring_on(k).wait_send()


def transform_tables():
    row = np.arange(512)
    h, xy, yy = row // 256, row // 16 % 16, row % 16
    used = (yy < 11).astype(np.float64)
    y = ((h * 16 + xy) * 8 - 1 + yy) % N
    k = np.arange(N)
    angle = 2 * np.pi * (k[:, None] * y[None, :] % N) / N
    cosine, sine = np.cos(angle) * used, np.sin(angle) * used
    forward = np.stack([cosine.reshape(2, 128, 2, N), sine.reshape(2, 128, 2, N)], axis=1)
    forward = forward.transpose(3, 0, 1, 2, 4).reshape(2, 2, 256, N)
    backward = np.stack([cosine.T.reshape(2, 4, 64, N), sine.T.reshape(2, 4, 64, N)], axis=2)
    backward = backward.reshape(2, 4, 128, N)
    angle = 2 * np.pi * (k[:, None] * k[None, :] % N) / N
    high, low = np_halves(np.concatenate([np.cos(angle), np.sin(angle)], axis=1))
    along = np.concatenate([high, low, high], axis=0)
    return np.stack(np_halves(forward)), along, np.stack(np_halves(backward))


def on_device(values, weights, anchors, counts, spectrum):
    dma = pltpu.SemaphoreType.DMA
    anywhere = pl.BlockSpec(memory_space=pl.ANY)
    tables = transform_tables()
    field = pltpu.VMEM((2, 4, 256, 128), F32)
    strided = pltpu.VMEM((2, 4, 272, 128), F32)
    share = pltpu.VMEM((8, 32, N), F32)
    return pl.pallas_call(
        whole_kernel,
        out_shape=jax.ShapeDtypeStruct(values.shape, F32),
        in_specs=[SM, VM, VM] + [anywhere] * 5,
        out_specs=VM,
        scratch_shapes=[
            pltpu.VMEM(weights.shape, F32),
            pltpu.VMEM(spectrum.shape, F32),
            *[pltpu.VMEM(t.shape, BF16) for t in tables],
            pltpu.VMEM((128, 64), F32),
            pltpu.VMEM((2, 8, 72, 128), F32),
            pltpu.VMEM((352, N), F32),
            strided,
            field,
            pltpu.VMEM((2, 256, 2 * N), F32),
            field,
            strided,
            pltpu.VMEM((352, 2 * N), BF16),
            share,
            share,
            share,
            share,
            dma((10,)),
            *[dma((8,))] * 4,
            *[dma((2, 16))] * 4,
            *[dma((8,))] * 4,
        ],
        compiler_params=pltpu.CompilerParams(
            collective_id=1, has_side_effects=True, vmem_limit_bytes=LIMIT
        ),
    )(counts, values, anchors, weights, spectrum, *tables)


def solution(mesh):
    placed = (
        P(None, ("slab", "pencil")),
        P(("slab", "pencil"), None),
        P(None, ("slab", "pencil")),
        P(("slab", "pencil")),
        P(("slab", "pencil"), None, None),
    )
    return jax.shard_map(
        on_device,
        mesh=mesh,
        in_specs=placed,
        out_specs=P(None, ("slab", "pencil")),
        check_vma=False,
    )
```
